128 devices in a mesh: dp: 16 (over z_lo, y, core), tensor: 8 (over x, z_hi).
Axes of the slice: x: 4, y: 4, z: 4 (z_hi: 2, z_lo: 2; z = z_hi * 2 + z_lo), core: 2. Of those that a mesh axis runs over, the one named last changes fastest.
Arguments:
- attn_heads: bfloat16 [16384, 4096], P('dp', 'tensor'), may hold values from -3 to 3
- out_weight: bfloat16 [4096, 4096], P('tensor'), may hold values from -0.09375 to 0.09375
- residual: bfloat16 [16384, 4096], P(('dp', 'tensor')), may hold values from -6 to 6
- norm_gain: float32 [4096], replicated, may hold values from 0.1 to 1.9
- expert_ids: int32 [16384, 8], P(('dp', 'tensor')), may hold values from 0 to 127, all different within a row; in each aligned block of 128 rows (0 to 127, 128 to 255, ...) at most 10 rows name the same one
- gate_probs: float32 [16384, 8], P(('dp', 'tensor')), may hold values from 0.25 to 1
- expert_gate: bfloat16 [128, 4096, 768], P(('dp', 'tensor')), may hold values from -0.09375 to 0.09375
- expert_up: bfloat16 [128, 4096, 768], P(('dp', 'tensor')), may hold values from -0.09375 to 0.09375
- expert_down: bfloat16 [128, 768, 4096], P(('dp', 'tensor')), may hold values from -0.21875 to 0.21875
Outputs:
- layer_out: bfloat16 [16384, 4096], P(('dp', 'tensor'))
The draws below stay inside these ranges and needn't reach their ends.
Inputs may be any that keep to these rules, and one draw needn't show every extreme that they name: `expert_ids`: each row names 8 different experts. Among the rows of one device (aligned blocks of 128 rows), no expert is named by more than 10 rows, a bound that some block reaches.
All inputs are finite; a program needn't handle non-finite values.
Results may differ from the reference program's by a relative error of at most 0.02.
Values may be sent and summed in bfloat16 or wider, within the bound.
No kernel may reach another device: no remote copies, remote signals or barrier semaphores. Data moves between devices by JAX's collectives and lax.ppermute only.
A program may use at most 128 MiB of HBM per device.

```python
import math
import jax
import jax.numpy as jnp
import numpy as np
from jax import lax

D = 4096
HD = 128
QH = 32
HID = 768
TOPK = 8
TOK_DEV = 128
EXPERTS = 128
CAP = 10
SEQ = 16384
N_TENSOR = 8


def shard_levels(own_key, dims, pieces, least, largest):
    gain = 1.0
    for axis_at, parts in pieces:
        draws = jax.random.uniform(jax.random.fold_in(jax.random.fold_in(own_key, 6), axis_at), (parts,), jnp.float32, least / len(pieces), largest / len(pieces))
        gain = gain * jnp.repeat(jnp.exp(draws), dims[axis_at] // parts).reshape((-1,) + (1,) * (len(dims) - 1 - axis_at))
    return gain


def deal_out(key, own, number, rows, amount, top, bound, lean):
    sequence = jax.random.permutation(key, amount)
    heavy_load, ordinary = load_shares(amount, rows * top, bound, lean, True), load_shares(amount, rows * top, bound, lean, False)
    places = jnp.arange(amount)

    def named(sizes, rotation):
        used = int((sizes > 0).sum())
        fixed = max(1, used // 4)
        moved = fixed + (places - fixed + rotation * (used - fixed)) % max(1, amount - fixed)
        return jnp.zeros((amount,), jnp.int32).at[sequence[jnp.where(places < fixed, places, moved)]].set(jnp.asarray(sizes, jnp.int32))

    sizes = jnp.where(number % 4 == 0, named(heavy_load, number // 4), named(ordinary, number - number // 4 - 1))
    mixed = jax.random.permutation(jax.random.fold_in(own, 3), amount)
    source_of, receiver = mixed[0:amount // 2 * 2:2], mixed[1:amount // 2 * 2:2]
    room = jnp.minimum(sizes[source_of] - 1, bound - sizes[receiver]) // 2
    room = jnp.where((source_of == sequence[0]) | (receiver == sequence[0]) | (sizes[receiver] == 0), 0, jnp.maximum(room, 0))
    moved = jax.random.randint(jax.random.fold_in(own, 4), (amount // 2,), 0, 1 << 20) % (room + 1)
    sizes = sizes.at[source_of].add(-moved).at[receiver].add(moved)
    members = jnp.searchsorted(jnp.cumsum(sizes), jnp.arange(rows * top), side="right").astype(jnp.int32)
    listing = members.reshape(top, rows).T
    listing = listing[jax.random.permutation(jax.random.fold_in(own, 1), rows)]
    rotation = jax.random.randint(jax.random.fold_in(own, 2), (rows, 1), 0, top)
    return jnp.take_along_axis(listing, (jnp.arange(top)[None, :] + rotation) % top, axis=1)


def load_shares(amount, total, reach, slope, full):
    portions = [(1 << 20) // math.isqrt(grade ** slope) + 1 for grade in range(1, amount + 1)]
    largest = reach if full else min(reach, max(-(-total // amount), total * portions[0] // sum(portions)))
    least = 1 if total - largest >= amount - 1 else 0
    holding, spare = [largest] + [least] * (amount - 1), total - largest - least * (amount - 1)
    while spare > 0:
        candidates = [i for i in range(1, amount) if holding[i] < largest] or [i for i in range(1, amount) if holding[i] < reach]
        mass, remaining = sum([portions[i] for i in candidates]), spare
        for i in candidates:
            more = min(reach - holding[i], max(1, remaining * portions[i] // mass), spare)
            holding[i] = holding[i] + more
            spare = spare - more
    return np.array(holding)


def normal_values(stream_key, shape, scale, reach, shards=(), kind=jnp.bfloat16):
    result = jax.random.normal(stream_key, shape, jnp.float32) * scale
    if len(shards) > 0:
        result = shard_levels(stream_key, shape, shards, -0.22, 0.18) * result
    return jnp.clip(result, min=-reach, max=reach).astype(kind)


def setup_inputs(seed: int = 0) -> dict:
    arg_keys = jax.random.split(jax.random.key(seed), 10)
    attn_heads = normal_values(arg_keys[0], (SEQ, QH * HD), 0.5, 3.0, ((0, 16), (1, 8)))
    out_weight = normal_values(arg_keys[1], (QH * HD, D), (QH * HD) ** -0.5, 0.09375, ((0, 8),))
    residual = normal_values(arg_keys[2], (SEQ, D), 1.0, 6.0, ((0, 128),))
    norm_gain = jnp.clip(1.0 + 0.18 * jax.random.normal(arg_keys[3], (D,), jnp.float32), 0.1, 1.9)
    expert_ids_keys = jax.random.split(jax.random.fold_in(arg_keys[4], 1), SEQ // TOK_DEV)
    expert_ids_turns = jax.random.permutation(jax.random.fold_in(arg_keys[4], 3), SEQ // TOK_DEV)
    expert_ids = jax.vmap(lambda own, number: deal_out(jax.random.fold_in(arg_keys[4], 2), own, number, TOK_DEV, EXPERTS, TOPK, CAP, 2))(expert_ids_keys, expert_ids_turns).reshape((SEQ, TOPK))
    gate_probs = jnp.clip(0.25 + 0.75 * jax.random.uniform(arg_keys[5], (SEQ, TOPK), jnp.float32) ** shard_levels(arg_keys[5], (SEQ, TOPK), ((0, 128),), -0.2, 0.2), 0.25, 1.0)
    expert_gate = normal_values(arg_keys[6], (EXPERTS, D, HID), D ** -0.5, 0.09375, ((0, 128),))
    expert_up = normal_values(arg_keys[7], (EXPERTS, D, HID), D ** -0.5, 0.09375, ((0, 128),))
    expert_down = normal_values(arg_keys[8], (EXPERTS, HID, D), HID ** -0.5, 0.21875, ((0, 128),))
    return dict(attn_heads=attn_heads, out_weight=out_weight, residual=residual, norm_gain=norm_gain, expert_ids=expert_ids, gate_probs=gate_probs, expert_gate=expert_gate, expert_up=expert_up, expert_down=expert_down)


def reference(attn_heads, out_weight, residual, norm_gain, expert_ids, gate_probs, expert_gate, expert_up, expert_down):
    seq_len = residual.shape[0]
    model_width = residual.shape[1]
    group_width = attn_heads.shape[1] // N_TENSOR
    attn_out = jnp.zeros((seq_len, model_width), jnp.float32)
    for column_group in range(N_TENSOR):
        first_col = column_group * group_width
        partial_sum = jnp.dot(attn_heads[:, first_col:first_col + group_width], out_weight[first_col:first_col + group_width], preferred_element_type=jnp.float32)
        rounded = lax.optimization_barrier(partial_sum.astype(jnp.bfloat16))
        attn_out = attn_out + rounded.astype(jnp.float32)
    hidden_state = residual.astype(jnp.float32) + attn_out
    inv_rms = lax.rsqrt(lax.optimization_barrier(jnp.mean(hidden_state * hidden_state, axis=1, keepdims=True)) + 1e-06)
    normed = (hidden_state * inv_rms * norm_gain).astype(jnp.bfloat16)
    blocks_count = seq_len // TOK_DEV
    block_ids = expert_ids.reshape(blocks_count, TOK_DEV * TOPK)
    expert_range = jnp.arange(EXPERTS, dtype=jnp.int32)
    onehot = (block_ids[:, :, None] == expert_range[None, None, :]).astype(jnp.int32)
    prior_count = jnp.cumsum(onehot, axis=1) - onehot
    slot_index = lax.optimization_barrier(jnp.sum(prior_count * onehot, axis=2))
    block_start = CAP * jnp.arange(blocks_count, dtype=jnp.int32)
    positions = (slot_index + block_start[:, None]).reshape(-1).astype(jnp.int32)
    flat_ids = expert_ids.reshape(-1).astype(jnp.int32)
    source_rows = (jnp.arange(seq_len * TOPK, dtype=jnp.int32) // TOPK).astype(jnp.int32)
    row_table = jnp.zeros((EXPERTS, blocks_count * CAP), jnp.int32).at[flat_ids, positions].set(source_rows)
    weight_table = jnp.zeros((EXPERTS, blocks_count * CAP), gate_probs.dtype).at[flat_ids, positions].set(gate_probs.reshape(-1))

    def serve(routed_sum, operands):
        table_rows, table_weights, w_gate, w_up, w_down = operands
        chosen = normed[table_rows]
        gate_act = jnp.dot(chosen, w_gate, preferred_element_type=jnp.float32)
        up_act = jnp.dot(chosen, w_up, preferred_element_type=jnp.float32)
        active = (jax.nn.silu(gate_act) * up_act).astype(jnp.bfloat16)
        expert_row = jnp.dot(active, w_down, preferred_element_type=jnp.float32).astype(jnp.bfloat16)
        contribution = table_weights[:, None] * expert_row.astype(jnp.float32)
        return (routed_sum.at[table_rows].add(contribution), None)
    start_sum = jnp.zeros((seq_len, model_width), jnp.float32)
    routed_sum, unused = lax.scan(serve, start_sum, (row_table, weight_table, expert_gate, expert_up, expert_down))
    return (hidden_state + routed_sum).astype(jnp.bfloat16)
```

```python
import jax
import jax.numpy as jnp
from jax import lax
from jax.sharding import PartitionSpec as P

F32, BF16 = jnp.float32, jnp.bfloat16
MAIN = 8
QUARTERS = 4


def route(expert_ids, gate_probs, experts):
    toks = expert_ids.shape[0]
    names = jnp.arange(experts, dtype=jnp.int32)
    chosen = expert_ids.T[:, None, :] == names[None, :, None]
    taken = jnp.any(chosen, axis=0)
    prob = jnp.sum(jnp.where(chosen, gate_probs.T[:, None, :], 0.0), axis=0)
    order = jnp.arange(toks)
    earlier = (order[:, None] < order[None, :]).astype(BF16)
    before = jnp.dot(taken.astype(BF16), earlier, preferred_element_type=F32)
    return jnp.where(taken, before.astype(jnp.int32), -1), prob


def expert_apply(rows, w_gate, w_up, w_down):
    gate_act = jnp.dot(rows, w_gate, preferred_element_type=F32)
    up_act = jnp.dot(rows, w_up, preferred_element_type=F32)
    active = (jax.nn.silu(gate_act) * up_act).astype(BF16)
    return jnp.dot(active, w_down, preferred_element_type=F32).astype(BF16)


def shards(attn_heads, out_weight, residual, norm_gain, expert_ids, gate_probs, expert_gate, expert_up, expert_down):
    toks, width = residual.shape
    axes = ("dp", "tensor")
    experts = lax.axis_size("dp") * lax.axis_size("tensor")
    quarter = width // QUARTERS
    slot, prob = route(expert_ids, gate_probs, experts)
    row = jnp.arange(MAIN, dtype=jnp.int32)
    main_hot = slot[:, None, :] == row[None, :, None]
    spill_hot = slot[:, None, :] == (MAIN + row // QUARTERS)[None, :, None]
    piece = (row % QUARTERS)[None, :, None]
    spill_parts = [spill_hot & (piece == c) for c in range(QUARTERS)]

    attn_out = lax.psum_scatter(
        jnp.dot(attn_heads, out_weight, preferred_element_type=F32).astype(BF16),
        "tensor",
        scatter_dimension=0,
        tiled=True,
    ).astype(F32)
    hidden_state = residual.astype(F32) + attn_out
    inv_rms = lax.rsqrt(jnp.mean(hidden_state * hidden_state, axis=1, keepdims=True) + 1e-06)
    normed = (hidden_state * inv_rms * norm_gain).astype(BF16)

    flat = experts * MAIN
    main_out = jnp.dot(main_hot.reshape(flat, toks).astype(BF16), normed, preferred_element_type=F32).astype(BF16)
    stacked = jnp.concatenate([normed[:, c * quarter : (c + 1) * quarter] for c in range(QUARTERS)], axis=0)
    spill_all = jnp.concatenate([s.reshape(flat, toks) for s in spill_parts], axis=1).astype(BF16)
    spill_out = jnp.dot(spill_all, stacked, preferred_element_type=F32).astype(BF16)

    def swap(x, cols):
        y = lax.all_to_all(x.reshape(experts, MAIN, cols), axes, split_axis=0, concat_axis=0, tiled=True)
        return y.reshape(flat, cols)

    main_in = swap(main_out, width)
    spill_in = swap(spill_out, quarter)
    w = (expert_gate[0], expert_up[0], expert_down[0])
    main_back = swap(expert_apply(main_in, *w), width)
    spill_back = swap(expert_apply(spill_in.reshape(-1, width), *w).reshape(flat, quarter), quarter)

    hi = prob.astype(BF16)
    lo = (prob - hi.astype(F32)).astype(BF16)
    both = jnp.concatenate([hi, lo], axis=1)

    def combine(hot, rows):
        hot2 = jnp.concatenate([hot, hot], axis=2)
        weight = jnp.where(hot2, both[:, None, :], jnp.zeros((), BF16)).reshape(flat, 2 * toks)
        out = lax.dot_general(weight, rows, (((0,), (0,)), ((), ())), preferred_element_type=F32)
        return out[:toks] + out[toks:]

    routed = combine(main_hot, main_back)
    routed = routed + jnp.concatenate([combine(s, spill_back) for s in spill_parts], axis=1)
    return (hidden_state + routed).astype(BF16)


def solution(mesh):
    both = ("dp", "tensor")
    in_specs = (
        P("dp", "tensor"),
        P("tensor", None),
        P(both, None),
        P(),
        P(both, None),
        P(both, None),
        P(both, None, None),
        P(both, None, None),
        P(both, None, None),
    )
    return jax.shard_map(shards, mesh=mesh, in_specs=in_specs, out_specs=P(both, None), check_vma=False)
```

```python
import jax
import jax.numpy as jnp
from jax import lax
from jax.sharding import PartitionSpec as P

F32, BF16 = jnp.float32, jnp.bfloat16
MAIN = 8
QUARTERS = 4


def route(expert_ids, gate_probs, experts):
    toks = expert_ids.shape[0]
    names = jnp.arange(experts, dtype=jnp.int32)
    chosen = expert_ids.T[:, None, :] == names[None, :, None]
    taken = jnp.any(chosen, axis=0)
    prob = jnp.sum(jnp.where(chosen, gate_probs.T[:, None, :], 0.0), axis=0)
    order = jnp.arange(toks)
    earlier = (order[:, None] < order[None, :]).astype(BF16)
    before = jnp.dot(taken.astype(BF16), earlier, preferred_element_type=F32)
    return jnp.where(taken, before.astype(jnp.int32), -1), prob


def expert_apply(rows, w_gate, w_up, w_down):
    gate_act = jnp.dot(rows, w_gate, preferred_element_type=F32)
    up_act = jnp.dot(rows, w_up, preferred_element_type=F32)
    active = (jax.nn.silu(gate_act) * up_act).astype(BF16)
    return jnp.dot(active, w_down, preferred_element_type=F32).astype(BF16)


def project_scatter(attn_heads, out_weight, toks):
    width = out_weight.shape[1]
    first = width * 5 // 8
    at = lax.axis_index("tensor")
    x, z = at // 2, at % 2
    heads = attn_heads.reshape(4, 2, toks, attn_heads.shape[1])

    def along_x(v, by):
        return lax.ppermute(v, "tensor", [(i * 2 + j, (i + by) % 4 * 2 + j) for i in range(4) for j in range(2)])

    def along_z(v):
        return lax.ppermute(v, "tensor", [(i, i ^ 1) for i in range(8)])

    def times(rows, lo, hi):
        return jnp.dot(rows, out_weight[:, lo:hi], preferred_element_type=F32).astype(BF16)

    def pick(v, i):
        return lax.dynamic_index_in_dim(v, i, 0, keepdims=False)

    def ring(chunk, lo, hi):
        mid = (lo + hi) // 2
        up_far = along_x(chunk(2, mid, hi), 1)
        down_far = along_x(chunk(2, lo, mid), -1)
        up_near = along_x(chunk(1, lo, mid), 1)
        down_near = along_x(chunk(-1, mid, hi), -1)
        up_sum = along_x((chunk(1, mid, hi).astype(F32) + up_far.astype(F32)).astype(BF16), 1)
        down_sum = along_x((chunk(-1, lo, mid).astype(F32) + down_far.astype(F32)).astype(BF16), -1)
        left = chunk(0, lo, mid).astype(F32) + up_near.astype(F32) + down_sum.astype(F32)
        right = chunk(0, mid, hi).astype(F32) + up_sum.astype(F32) + down_near.astype(F32)
        return jnp.concatenate([left, right], axis=1)

    away = along_z(times(pick(heads.swapaxes(0, 1), 1 - z).reshape(4 * toks, -1), first, width))
    near_sum = ring(lambda d, lo, hi: times(pick(heads, (x + d) % 4).reshape(2 * toks, -1), lo, hi), 0, first)
    near_sum = near_sum.reshape(2, toks, first)
    near = pick(near_sum, z) + along_z(pick(near_sum, 1 - z).astype(BF16)).astype(F32)

    own = times(pick(heads.swapaxes(0, 1), z).reshape(4 * toks, -1), first, width)
    both = (own.astype(F32) + away.astype(F32)).astype(BF16).reshape(4, toks, width - first)
    far = ring(lambda d, lo, hi: pick(both, (x + d) % 4)[:, lo:hi], 0, width - first)
    return near, far


def shards(attn_heads, out_weight, residual, norm_gain, expert_ids, gate_probs, expert_gate, expert_up, expert_down):
    toks, width = residual.shape
    axes = ("dp", "tensor")
    experts = lax.axis_size("dp") * lax.axis_size("tensor")
    quarter = width // QUARTERS
    slot, prob = route(expert_ids, gate_probs, experts)
    row = jnp.arange(MAIN, dtype=jnp.int32)
    main_hot = slot[:, None, :] == row[None, :, None]
    spill_hot = slot[:, None, :] == (MAIN + row // QUARTERS)[None, :, None]
    piece = (row % QUARTERS)[None, :, None]
    spill_parts = [spill_hot & (piece == c) for c in range(QUARTERS)]

    attn_out = jnp.concatenate(project_scatter(attn_heads, out_weight, toks), axis=1)
    hidden_state = residual.astype(F32) + attn_out
    inv_rms = lax.rsqrt(jnp.mean(hidden_state * hidden_state, axis=1, keepdims=True) + 1e-06)
    normed = (hidden_state * inv_rms * norm_gain).astype(BF16)

    flat = experts * MAIN
    main_out = jnp.dot(main_hot.reshape(flat, toks).astype(BF16), normed, preferred_element_type=F32).astype(BF16)
    stacked = jnp.concatenate([normed[:, c * quarter : (c + 1) * quarter] for c in range(QUARTERS)], axis=0)
    spill_all = jnp.concatenate([s.reshape(flat, toks) for s in spill_parts], axis=1).astype(BF16)
    spill_out = jnp.dot(spill_all, stacked, preferred_element_type=F32).astype(BF16)

    def swap(x, cols):
        y = lax.all_to_all(x.reshape(experts, MAIN, cols), axes, split_axis=0, concat_axis=0, tiled=True)
        return y.reshape(flat, cols)

    main_in = swap(main_out, width)
    spill_in = swap(spill_out, quarter)
    w = (expert_gate[0], expert_up[0], expert_down[0])
    main_back = swap(expert_apply(main_in, *w), width)
    spill_back = swap(expert_apply(spill_in.reshape(-1, width), *w).reshape(flat, quarter), quarter)

    hi = prob.astype(BF16)
    lo = (prob - hi.astype(F32)).astype(BF16)
    both = jnp.concatenate([hi, lo], axis=1)

    def combine(hot, rows):
        hot2 = jnp.concatenate([hot, hot], axis=2)
        weight = jnp.where(hot2, both[:, None, :], jnp.zeros((), BF16)).reshape(flat, 2 * toks)
        out = lax.dot_general(weight, rows, (((0,), (0,)), ((), ())), preferred_element_type=F32)
        return out[:toks] + out[toks:]

    routed = combine(main_hot, main_back)
    routed = routed + jnp.concatenate([combine(s, spill_back) for s in spill_parts], axis=1)
    return (hidden_state + routed).astype(BF16)


def solution(mesh):
    both = ("dp", "tensor")
    in_specs = (
        P("dp", "tensor"),
        P("tensor", None),
        P(both, None),
        P(),
        P(both, None),
        P(both, None),
        P(both, None, None),
        P(both, None, None),
        P(both, None, None),
    )
    return jax.shard_map(shards, mesh=mesh, in_specs=in_specs, out_specs=P(both, None), check_vma=False)
```

```python
import jax
import jax.numpy as jnp
from jax import lax
from jax.experimental import pallas as pl
from jax.experimental.pallas import tpu as pltpu
from jax.sharding import PartitionSpec as P

F32, BF16 = jnp.float32, jnp.bfloat16
MAIN = 8
PIECES = 4
VMEM = 40 * 2**20


def dot(a, b):
    return jnp.dot(a, b, preferred_element_type=F32)


def route(expert_ids, gate_probs, experts):
    toks = expert_ids.shape[0]
    names = jnp.arange(experts, dtype=jnp.int32)
    chosen = expert_ids.T[:, None, :] == names[None, :, None]
    taken = jnp.any(chosen, axis=0)
    prob = jnp.sum(jnp.where(chosen, gate_probs.T[:, None, :], 0.0), axis=0)
    order = jnp.arange(toks)
    earlier = (order[:, None] < order[None, :]).astype(BF16)
    before = dot(taken.astype(BF16), earlier)
    return jnp.where(taken, before.astype(jnp.int32), -1), prob


def combine_weights(slot, prob):
    experts, toks = slot.shape
    hi = prob.astype(BF16)
    lo = (prob - hi.astype(F32)).astype(BF16)
    both = jnp.concatenate([hi, lo], axis=1)
    row = jnp.arange(MAIN, dtype=jnp.int32)

    def spread(names):
        hot = slot[:, None, :] == names[None, :, None]
        hot = jnp.concatenate([hot, hot], axis=2)
        return jnp.where(hot, both[:, None, :], jnp.zeros((), BF16)).reshape(experts * MAIN, 2 * toks).T

    return spread(row), spread(MAIN + row // PIECES)


def build(slot, near, far, residual, gain):
    experts, toks = slot.shape
    width = residual.shape[1]
    tile = width // PIECES
    flat = experts * MAIN
    first = near.shape[1]

    def kernel(slot_ref, near_ref, far_ref, residual_ref, gain_ref, out_ref, hidden_ref, normed):
        step = pl.program_id(0)

        @pl.when(step == 0)
        def _():
            hidden_ref[:, :first] = residual_ref[:, :first].astype(F32) + near_ref[...]
            hidden_ref[:, first:] = residual_ref[:, first:].astype(F32) + far_ref[...]
            hidden = hidden_ref[...]
            inv_rms = lax.rsqrt(jnp.mean(hidden * hidden, axis=1, keepdims=True) + 1e-06)
            value = (hidden * inv_rms * gain_ref[...]).astype(BF16)
            for c in range(PIECES):
                normed[c] = value[:, c * tile : (c + 1) * tile]

        slots = jnp.broadcast_to(slot_ref[...][:, None, :], (experts, MAIN, toks))
        row = lax.broadcasted_iota(jnp.int32, (experts, MAIN, toks), 1)

        def hot(mask):
            return jnp.where(mask, 1.0, 0.0).reshape(flat, toks).astype(BF16)

        @pl.when(step < PIECES)
        def _():
            out_ref[...] = dot(hot(slots == row), normed[step]).astype(BF16)

        @pl.when(step == PIECES)
        def _():
            spill = slots == MAIN + row // PIECES
            total = jnp.zeros((flat, tile), F32)
            for c in range(PIECES):
                total = total + dot(hot(spill & (row % PIECES == c)), normed[c])
            out_ref[...] = total.astype(BF16)

    whole = lambda i: (0, 0)
    return pl.pallas_call(
        kernel,
        grid=(PIECES + 1,),
        in_specs=[
            pl.BlockSpec(slot.shape, whole),
            pl.BlockSpec(near.shape, whole),
            pl.BlockSpec(far.shape, whole),
            pl.BlockSpec(residual.shape, whole),
            pl.BlockSpec(gain.shape, whole),
        ],
        out_specs=[pl.BlockSpec((flat, tile), lambda i: (0, i)), pl.BlockSpec((toks, width), whole)],
        out_shape=[
            jax.ShapeDtypeStruct((flat, tile * (PIECES + 1)), BF16),
            jax.ShapeDtypeStruct((toks, width), F32),
        ],
        scratch_shapes=[pltpu.VMEM((PIECES, toks, tile), BF16)],
        compiler_params=pltpu.CompilerParams(vmem_limit_bytes=VMEM),
        cost_estimate=pl.CostEstimate(flops=3 * 10**9, bytes_accessed=15 * 10**6, transcendentals=0),
        name="build_rows",
    )(slot, near, far, residual, gain)


def silu_times(gate, up):
    return (gate * jax.nn.sigmoid(gate) * up).astype(BF16)


def spill_expert(got, w_gate, w_up, w_down):
    flat, columns = got.shape
    hid = w_gate.shape[1]
    tile = columns // (PIECES + 1)
    rows = flat // PIECES

    def picks(c, shape, out_dim):
        out = lax.broadcasted_iota(jnp.int32, shape, out_dim)
        source = lax.broadcasted_iota(jnp.int32, shape, 1 - out_dim)
        return jnp.where(source == out * PIECES + c, 1.0, 0.0).astype(BF16)

    def kernel(got_ref, gate_ref, up_ref, down_ref, out_ref, gate_sum, up_sum, active, total):
        step = pl.program_id(0)

        @pl.when(step == 0)
        def _():
            gate_sum[...] = jnp.zeros_like(gate_sum)
            up_sum[...] = jnp.zeros_like(up_sum)
            total[...] = jnp.zeros_like(total)

        @pl.when(step < PIECES)
        def _():
            value = dot(picks(step, (rows, flat), 0), got_ref[...]).astype(BF16)
            gate_sum[...] += dot(value, gate_ref[...])
            up_sum[...] += dot(value, up_ref[...])

        @pl.when(step == PIECES)
        def _():
            active[...] = silu_times(gate_sum[...], up_sum[...])

        @pl.when(step >= PIECES)
        def _():
            value = dot(active[...], down_ref[...]).astype(BF16)
            total[...] += dot(picks(step - PIECES, (flat, rows), 1), value)

        @pl.when(step == 2 * PIECES - 1)
        def _():
            out_ref[...] = total[...].astype(BF16)

    early = lambda i: (jnp.minimum(i, PIECES - 1), 0)
    return pl.pallas_call(
        kernel,
        grid=(2 * PIECES,),
        in_specs=[
            pl.BlockSpec((flat, tile), lambda i: (0, PIECES)),
            pl.BlockSpec((tile, hid), early),
            pl.BlockSpec((tile, hid), early),
            pl.BlockSpec((hid, tile), lambda i: (0, jnp.maximum(i - PIECES, 0))),
        ],
        out_specs=pl.BlockSpec((flat, tile), lambda i: (0, 0)),
        out_shape=jax.ShapeDtypeStruct((flat, tile), BF16),
        scratch_shapes=[
            pltpu.VMEM((rows, hid), F32),
            pltpu.VMEM((rows, hid), F32),
            pltpu.VMEM((rows, hid), BF16),
            pltpu.VMEM((flat, tile), F32),
        ],
        compiler_params=pltpu.CompilerParams(vmem_limit_bytes=63 * 2**20),
        cost_estimate=pl.CostEstimate(flops=9 * 10**9, bytes_accessed=23 * 10**6, transcendentals=0),
        name="spill_expert",
    )(got, w_gate, w_up, w_down)


def main_expert(got, w_gate, w_up, w_down):
    width, hid = w_gate.shape
    flat = got.shape[0]
    block = 256

    def kernel(rows_ref, gate_ref, up_ref, down_ref, out_ref):
        rows = rows_ref[...]
        active = silu_times(dot(rows, gate_ref[...]), dot(rows, up_ref[...]))
        out_ref[...] = dot(active, down_ref[...]).astype(BF16)

    whole = lambda i: (0, 0)
    once = pl.Buffered(1)
    return pl.pallas_call(
        kernel,
        grid=(flat // block,),
        in_specs=[
            pl.BlockSpec((block, width), lambda i: (i, 0)),
            pl.BlockSpec((width, hid), whole, pipeline_mode=once),
            pl.BlockSpec((width, hid), whole, pipeline_mode=once),
            pl.BlockSpec((hid, width), whole, pipeline_mode=once),
        ],
        out_specs=pl.BlockSpec((block, width), lambda i: (i, 0)),
        out_shape=jax.ShapeDtypeStruct((flat, width), BF16),
        compiler_params=pltpu.CompilerParams(vmem_limit_bytes=VMEM),
        cost_estimate=pl.CostEstimate(flops=20 * 10**9, bytes_accessed=36 * 10**6, transcendentals=10**6),
        name="main_expert",
    )(got, w_gate, w_up, w_down)


def combine(main_w, spill_w, main_rows, spill_rows, hidden):
    toks, width = hidden.shape
    flat = main_rows.shape[0]
    quarter = spill_rows.shape[1]
    halves = 2
    tile = quarter // halves

    def kernel(main_w_ref, spill_w_ref, main_ref, spill_ref, hidden_ref, out_ref):
        piece = pl.program_id(0) // halves
        column = lax.broadcasted_iota(jnp.int32, (2 * toks, flat), 1)
        spill = jnp.where(column % PIECES == piece, spill_w_ref[...].astype(F32), 0.0).astype(BF16)
        both = dot(main_w_ref[...], main_ref[...]) + dot(spill, spill_ref[...])
        out_ref[...] = (hidden_ref[...] + (both[:toks] + both[toks:])).astype(BF16)

    whole = lambda i: (0, 0)
    along = lambda i: (0, i)
    return pl.pallas_call(
        kernel,
        grid=(PIECES * halves,),
        in_specs=[
            pl.BlockSpec((2 * toks, flat), whole),
            pl.BlockSpec((2 * toks, flat), whole),
            pl.BlockSpec((flat, tile), along),
            pl.BlockSpec((flat, tile), lambda i: (0, i % halves)),
            pl.BlockSpec((toks, tile), along),
        ],
        out_specs=pl.BlockSpec((toks, tile), along),
        out_shape=jax.ShapeDtypeStruct((toks, width), BF16),
        compiler_params=pltpu.CompilerParams(vmem_limit_bytes=VMEM),
        cost_estimate=pl.CostEstimate(flops=4 * 10**9, bytes_accessed=15 * 10**6, transcendentals=0),
        name="combine_rows",
    )(main_w, spill_w, main_rows, spill_rows, hidden)


def project_scatter(attn_heads, out_weight, toks):
    width = out_weight.shape[1]
    first = width * 5 // 8
    at = lax.axis_index("tensor")
    x, z = at // 2, at % 2
    heads = attn_heads.reshape(4, 2, toks, attn_heads.shape[1])

    def along_x(v, by):
        return lax.ppermute(v, "tensor", [(i * 2 + j, (i + by) % 4 * 2 + j) for i in range(4) for j in range(2)])

    def along_z(v):
        return lax.ppermute(v, "tensor", [(i, i ^ 1) for i in range(8)])

    def times(rows, lo, hi):
        return dot(rows, out_weight[:, lo:hi]).astype(BF16)

    def pick(v, i):
        return lax.dynamic_index_in_dim(v, i, 0, keepdims=False)

    def add(a, b):
        return (a.astype(F32) + b.astype(F32)).astype(BF16)

    by_z = heads.swapaxes(0, 1)
    far_rows = [pick(heads, (x + d) % 4).reshape(2 * toks, -1) for d in range(4)]
    mid = first // 2

    up_two, down_two = times(far_rows[2], mid, first), times(far_rows[2], 0, mid)
    z_rows = pick(by_z, 1 - z).reshape(4 * toks, -1)
    up_two, down_two, z_rows = lax.optimization_barrier((up_two, down_two, z_rows))
    up_far, down_far = along_x(up_two, 1), along_x(down_two, -1)
    away = along_z(times(z_rows, first, width))
    up_near = along_x(times(far_rows[1], 0, mid), 1)
    down_near = along_x(times(far_rows[3], mid, first), -1)
    up_sum = along_x(add(dot(far_rows[1], out_weight[:, mid:first]).astype(BF16), up_far), 1)
    down_sum = along_x(add(dot(far_rows[3], out_weight[:, :mid]).astype(BF16), down_far), -1)

    own = times(pick(by_z, z).reshape(4 * toks, -1), first, width)
    both = add(own, away)
    both, own_rows = lax.optimization_barrier((both, far_rows[0]))
    both = both.reshape(4, toks, width - first)
    chunk = [pick(both, (x + d) % 4) for d in range(4)]
    half = (width - first) // 2
    b_up_far, b_down_far = along_x(chunk[2][:, half:], 1), along_x(chunk[2][:, :half], -1)
    b_up_near, b_down_near = along_x(chunk[1][:, :half], 1), along_x(chunk[3][:, half:], -1)
    b_up_sum = along_x(add(chunk[1][:, half:], b_up_far), 1)
    b_down_sum = along_x(add(chunk[3][:, :half], b_down_far), -1)

    left = times(own_rows, 0, mid).astype(F32) + up_near.astype(F32) + down_sum.astype(F32)
    right = times(own_rows, mid, first).astype(F32) + up_sum.astype(F32) + down_near.astype(F32)
    near = jnp.concatenate([left, right], axis=1).reshape(2, toks, first)
    near = pick(near, z) + along_z(pick(near, 1 - z).astype(BF16)).astype(F32)
    b_left = chunk[0][:, :half].astype(F32) + b_up_near.astype(F32) + b_down_sum.astype(F32)
    b_right = chunk[0][:, half:].astype(F32) + b_up_sum.astype(F32) + b_down_near.astype(F32)
    return near, jnp.concatenate([b_left, b_right], axis=1)


def shards(attn_heads, out_weight, residual, norm_gain, expert_ids, gate_probs, expert_gate, expert_up, expert_down):
    toks, width = residual.shape
    experts = lax.axis_size("dp") * lax.axis_size("tensor")
    flat = experts * MAIN
    slot, prob = route(expert_ids, gate_probs, experts)
    main_w, spill_w = combine_weights(slot, prob)
    near, far = project_scatter(attn_heads, out_weight, toks)
    sent, hidden = build(slot, near, far, residual, norm_gain[None, :])

    def swap(v):
        cols = v.shape[1]
        v = lax.all_to_all(v.reshape(experts, MAIN, cols), ("dp", "tensor"), split_axis=0, concat_axis=0, tiled=True)
        return v.reshape(flat, cols)

    got = swap(sent)
    w = (expert_gate[0], expert_up[0], expert_down[0])
    spill_out = spill_expert(got, *w)
    spill_out, got = lax.optimization_barrier((spill_out, got))
    spill_back = swap(spill_out)
    main_back = swap(main_expert(got, *w))
    return combine(main_w, spill_w, main_back, spill_back, hidden)


def solution(mesh):
    both = ("dp", "tensor")
    in_specs = (
        P("dp", "tensor"),
        P("tensor", None),
        P(both, None),
        P(),
        P(both, None),
        P(both, None),
        P(both, None, None),
        P(both, None, None),
        P(both, None, None),
    )
    return jax.shard_map(shards, mesh=mesh, in_specs=in_specs, out_specs=P(both, None), check_vma=False)
```

```python
import jax
import jax.numpy as jnp
from jax import lax
from jax.experimental import pallas as pl
from jax.experimental.pallas import tpu as pltpu
from jax.sharding import PartitionSpec as P

F32, BF16 = jnp.float32, jnp.bfloat16
MAIN = 8
PIECES = 4
LANES = 128
VMEM = 40 * 2**20


def dot(a, b):
    return jnp.dot(a, b, preferred_element_type=F32)


def route(expert_ids, gate_probs, experts):
    toks = expert_ids.shape[0]
    names = jnp.arange(experts, dtype=jnp.int32)
    chosen = expert_ids.T[:, None, :] == names[None, :, None]
    taken = jnp.any(chosen, axis=0)
    prob = jnp.sum(jnp.where(chosen, gate_probs.T[:, None, :], 0.0), axis=0)
    order = jnp.arange(toks)
    earlier = (order[:, None] < order[None, :]).astype(BF16)
    before = dot(taken.astype(BF16), earlier)
    return jnp.where(taken, before.astype(jnp.int32), -1), prob


def combine_weights(slot, prob):
    experts, toks = slot.shape
    hi = prob.astype(BF16)
    lo = (prob - hi.astype(F32)).astype(BF16)
    both = jnp.concatenate([hi, lo], axis=1)

    def spread(names):
        hot = slot[:, None, :] == names[None, :, None]
        hot = jnp.concatenate([hot, hot], axis=2)
        return jnp.where(hot, both[:, None, :], jnp.zeros((), BF16)).reshape(experts * names.size, 2 * toks).T

    return spread(jnp.arange(MAIN, dtype=jnp.int32)), spread(MAIN + jnp.arange(MAIN // PIECES, dtype=jnp.int32))


def build(slot, near, far, residual, gain):
    experts, toks = slot.shape
    width = residual.shape[1]
    tile = width // PIECES
    flat = experts * MAIN
    first = near.shape[1]

    def kernel(slot_ref, near_ref, far_ref, residual_ref, gain_ref, out_ref, hidden_ref, normed):
        step = pl.program_id(0)

        @pl.when(step == 0)
        def _():
            hidden_ref[:, :first] = residual_ref[:, :first].astype(F32) + near_ref[...]
            hidden_ref[:, first:] = residual_ref[:, first:].astype(F32) + far_ref[...]
            hidden = hidden_ref[...]
            inv_rms = lax.rsqrt(jnp.mean(hidden * hidden, axis=1, keepdims=True) + 1e-06)
            value = (hidden * inv_rms * gain_ref[...]).astype(BF16)
            for c in range(PIECES):
                normed[c] = value[:, c * tile : (c + 1) * tile]

        slots = jnp.broadcast_to(slot_ref[...][:, None, :], (experts, MAIN, toks))
        row = lax.broadcasted_iota(jnp.int32, (experts, MAIN, toks), 1)

        def hot(mask):
            return jnp.where(mask, 1.0, 0.0).reshape(flat, toks).astype(BF16)

        @pl.when(step < PIECES)
        def _():
            out_ref[...] = dot(hot(slots == row), normed[step]).astype(BF16)

        @pl.when(step == PIECES)
        def _():
            spill = slots == MAIN + row // PIECES
            parts = [hot(spill & (row % PIECES == c)) for c in range(PIECES)]
            out_ref[...] = dot(jnp.concatenate(parts, axis=1), normed[...].reshape(PIECES * toks, tile)).astype(BF16)

    whole = lambda i: (0, 0)
    return pl.pallas_call(
        kernel,
        grid=(PIECES + 1,),
        in_specs=[
            pl.BlockSpec(slot.shape, whole),
            pl.BlockSpec(near.shape, whole),
            pl.BlockSpec(far.shape, whole),
            pl.BlockSpec(residual.shape, whole),
            pl.BlockSpec(gain.shape, whole),
        ],
        out_specs=[pl.BlockSpec((flat, tile), lambda i: (0, i)), pl.BlockSpec((toks, width), whole)],
        out_shape=[
            jax.ShapeDtypeStruct((flat, tile * (PIECES + 1)), BF16),
            jax.ShapeDtypeStruct((toks, width), F32),
        ],
        scratch_shapes=[pltpu.VMEM((PIECES, toks, tile), BF16)],
        compiler_params=pltpu.CompilerParams(vmem_limit_bytes=VMEM),
        cost_estimate=pl.CostEstimate(flops=3 * 10**9, bytes_accessed=15 * 10**6, transcendentals=0),
        name="build_rows",
    )(slot, near, far, residual, gain)


def silu_times(gate, up):
    return (gate * jax.nn.sigmoid(gate) * up).astype(BF16)


def expert(got, w_gate, w_up, w_down, block=256):
    flat, columns = got.shape
    width, hid = w_gate.shape
    tile = columns - width
    extra = block // PIECES

    def kernel(got_ref, gate_ref, up_ref, down_ref, out_ref, rows, spill):
        rows[:block] = got_ref[:, :width]
        for c in range(tile // LANES):
            spill[c] = got_ref[:, width + c * LANES : width + (c + 1) * LANES].astype(F32)
        for c in range(PIECES):
            for d in range(tile // LANES):
                at = c * tile + d * LANES
                rows[block:, at : at + LANES] = spill[d, pl.ds(c, extra, stride=PIECES), :].astype(BF16)
        value = rows[...]
        active = silu_times(dot(value, gate_ref[...]), dot(value, up_ref[...]))
        for c in range(PIECES):
            cols = slice(c * tile, (c + 1) * tile)
            made = dot(active, down_ref[:, cols])
            out_ref[:, cols] = made[:block].astype(BF16)
            for d in range(tile // LANES):
                spill[d, pl.ds(c, extra, stride=PIECES), :] = made[block:, d * LANES : (d + 1) * LANES]
        for d in range(tile // LANES):
            out_ref[:, width + d * LANES : width + (d + 1) * LANES] = spill[d].astype(BF16)

    whole = lambda i: (0, 0)
    once = pl.Buffered(1)
    return pl.pallas_call(
        kernel,
        grid=(flat // block,),
        in_specs=[
            pl.BlockSpec((block, columns), lambda i: (i, 0)),
            pl.BlockSpec((width, hid), whole, pipeline_mode=once),
            pl.BlockSpec((width, hid), whole, pipeline_mode=once),
            pl.BlockSpec((hid, width), whole, pipeline_mode=once),
        ],
        out_specs=pl.BlockSpec((block, columns), lambda i: (i, 0)),
        out_shape=jax.ShapeDtypeStruct((flat, columns), BF16),
        scratch_shapes=[
            pltpu.VMEM((block + extra, width), BF16),
            pltpu.VMEM((tile // LANES, block, LANES), F32),
        ],
        compiler_params=pltpu.CompilerParams(vmem_limit_bytes=VMEM),
        cost_estimate=pl.CostEstimate(flops=24 * 10**9, bytes_accessed=40 * 10**6, transcendentals=10**6),
        name="expert_rows",
    )(got, w_gate, w_up, w_down)


def combine(main_w, spill_w, back, hidden):
    toks, width = hidden.shape
    flat = back.shape[0]
    halves = 2
    tile = (back.shape[1] - width) // halves
    tiles = width // tile

    few = flat // PIECES

    def kernel(main_w_ref, spill_w_ref, main_ref, spill_ref, hidden_ref, out_ref, spill, rows):
        piece = pl.program_id(1)

        @pl.when(piece == 0)
        def _():
            for d in range(tile // LANES):
                spill[d] = spill_ref[:, d * LANES : (d + 1) * LANES].astype(F32)
            for c in range(PIECES):
                for d in range(tile // LANES):
                    picked = spill[d, pl.ds(c, few, stride=PIECES), :]
                    rows[c, :, d * LANES : (d + 1) * LANES] = picked.astype(BF16)

        both = dot(main_w_ref[...], main_ref[...]) + dot(spill_w_ref[...], rows[piece])
        out_ref[...] = (hidden_ref[...] + (both[:toks] + both[toks:])).astype(BF16)

    along = lambda half, piece: (0, piece * halves + half)
    return pl.pallas_call(
        kernel,
        grid=(halves, PIECES),
        in_specs=[
            pl.BlockSpec((2 * toks, flat), lambda half, piece: (0, 0)),
            pl.BlockSpec((2 * toks, few), lambda half, piece: (0, 0)),
            pl.BlockSpec((flat, tile), along),
            pl.BlockSpec((flat, tile), lambda half, piece: (0, tiles + half)),
            pl.BlockSpec((toks, tile), along),
        ],
        out_specs=pl.BlockSpec((toks, tile), along),
        out_shape=jax.ShapeDtypeStruct((toks, width), BF16),
        scratch_shapes=[
            pltpu.VMEM((tile // LANES, flat, LANES), F32),
            pltpu.VMEM((PIECES, few, tile), BF16),
        ],
        compiler_params=pltpu.CompilerParams(vmem_limit_bytes=63 * 2**20),
        cost_estimate=pl.CostEstimate(flops=4 * 10**9, bytes_accessed=15 * 10**6, transcendentals=0),
        name="combine_rows",
    )(main_w, spill_w, back, back, hidden)


def project_scatter(attn_heads, out_weight, toks):
    width = out_weight.shape[1]
    first = width * 5 // 8
    at = lax.axis_index("tensor")
    x, z = at // 2, at % 2
    heads = attn_heads.reshape(4, 2, toks, attn_heads.shape[1])

    def along_x(v, by):
        return lax.ppermute(v, "tensor", [(i * 2 + j, (i + by) % 4 * 2 + j) for i in range(4) for j in range(2)])

    def along_z(v):
        return lax.ppermute(v, "tensor", [(i, i ^ 1) for i in range(8)])

    def times(rows, lo, hi):
        return dot(rows, out_weight[:, lo:hi]).astype(BF16)

    def pick(v, i):
        return lax.dynamic_index_in_dim(v, i, 0, keepdims=False)

    def add(a, b):
        return (a.astype(F32) + b.astype(F32)).astype(BF16)

    by_z = heads.swapaxes(0, 1)
    far_rows = [pick(heads, (x + d) % 4).reshape(2 * toks, -1) for d in range(4)]
    mid = first // 2

    up_two, down_two = times(far_rows[2], mid, first), times(far_rows[2], 0, mid)
    z_rows = pick(by_z, 1 - z).reshape(4 * toks, -1)
    up_two, down_two, z_rows = lax.optimization_barrier((up_two, down_two, z_rows))
    up_far, down_far = along_x(up_two, 1), along_x(down_two, -1)
    away = along_z(times(z_rows, first, width))
    up_near = along_x(times(far_rows[1], 0, mid), 1)
    down_near = along_x(times(far_rows[3], mid, first), -1)
    up_sum = along_x(add(dot(far_rows[1], out_weight[:, mid:first]).astype(BF16), up_far), 1)
    down_sum = along_x(add(dot(far_rows[3], out_weight[:, :mid]).astype(BF16), down_far), -1)

    own = times(pick(by_z, z).reshape(4 * toks, -1), first, width)
    both = add(own, away)
    both, own_rows = lax.optimization_barrier((both, far_rows[0]))
    both = both.reshape(4, toks, width - first)
    chunk = [pick(both, (x + d) % 4) for d in range(4)]
    half = (width - first) // 2
    b_up_far, b_down_far = along_x(chunk[2][:, half:], 1), along_x(chunk[2][:, :half], -1)
    b_up_near, b_down_near = along_x(chunk[1][:, :half], 1), along_x(chunk[3][:, half:], -1)
    b_up_sum = along_x(add(chunk[1][:, half:], b_up_far), 1)
    b_down_sum = along_x(add(chunk[3][:, :half], b_down_far), -1)

    left = times(own_rows, 0, mid).astype(F32) + up_near.astype(F32) + down_sum.astype(F32)
    right = times(own_rows, mid, first).astype(F32) + up_sum.astype(F32) + down_near.astype(F32)
    near = jnp.concatenate([left, right], axis=1).reshape(2, toks, first)
    near = pick(near, z) + along_z(pick(near, 1 - z).astype(BF16)).astype(F32)
    b_left = chunk[0][:, :half].astype(F32) + b_up_near.astype(F32) + b_down_sum.astype(F32)
    b_right = chunk[0][:, half:].astype(F32) + b_up_sum.astype(F32) + b_down_near.astype(F32)
    return near, jnp.concatenate([b_left, b_right], axis=1)


def shards(attn_heads, out_weight, residual, norm_gain, expert_ids, gate_probs, expert_gate, expert_up, expert_down):
    toks, width = residual.shape
    experts = lax.axis_size("dp") * lax.axis_size("tensor")
    flat = experts * MAIN
    slot, prob = route(expert_ids, gate_probs, experts)
    main_w, spill_w = combine_weights(slot, prob)
    near, far = project_scatter(attn_heads, out_weight, toks)
    sent, hidden = build(slot, near, far, residual, norm_gain[None, :])

    def swap(v):
        cols = v.shape[1]
        v = lax.all_to_all(v.reshape(experts, MAIN, cols), ("dp", "tensor"), split_axis=0, concat_axis=0, tiled=True)
        return v.reshape(flat, cols)

    made = expert(swap(sent), expert_gate[0], expert_up[0], expert_down[0])
    return combine(main_w, spill_w, swap(made), hidden)


def solution(mesh):
    both = ("dp", "tensor")
    in_specs = (
        P("dp", "tensor"),
        P("tensor", None),
        P(both, None),
        P(),
        P(both, None),
        P(both, None),
        P(both, None, None),
        P(both, None, None),
        P(both, None, None),
    )
    return jax.shard_map(shards, mesh=mesh, in_specs=in_specs, out_specs=P(both, None), check_vma=False)
```

```python
import jax
import jax.numpy as jnp
from jax import lax
from jax.experimental import pallas as pl
from jax.experimental.pallas import tpu as pltpu
from jax.sharding import PartitionSpec as P

F32, BF16 = jnp.float32, jnp.bfloat16
MAIN = 8
PIECES = 4
LANES = 128
VMEM = 40 * 2**20


def dot(a, b):
    return jnp.dot(a, b, preferred_element_type=F32)


def route(expert_ids, gate_probs, experts):
    toks = expert_ids.shape[0]
    names = jnp.arange(experts, dtype=jnp.int32)
    chosen = expert_ids.T[:, None, :] == names[None, :, None]
    taken = jnp.any(chosen, axis=0)
    prob = jnp.sum(jnp.where(chosen, gate_probs.T[:, None, :], 0.0), axis=0)
    order = jnp.arange(toks)
    earlier = (order[:, None] < order[None, :]).astype(BF16)
    before = dot(taken.astype(BF16), earlier)
    return jnp.where(taken, before.astype(jnp.int32), -1), prob


def combine_weights(slot, prob):
    experts, toks = slot.shape
    hi = prob.astype(BF16)
    lo = (prob - hi.astype(F32)).astype(BF16)
    both = jnp.concatenate([hi, lo], axis=1)

    def spread(names):
        hot = slot[:, None, :] == names[None, :, None]
        hot = jnp.concatenate([hot, hot], axis=2)
        return jnp.where(hot, both[:, None, :], jnp.zeros((), BF16)).reshape(experts * names.size, 2 * toks).T

    return spread(jnp.arange(MAIN, dtype=jnp.int32)), spread(MAIN + jnp.arange(MAIN // PIECES, dtype=jnp.int32))


def build(slot, near, far, residual, gain):
    experts, toks = slot.shape
    width = residual.shape[1]
    tile = width // PIECES
    flat = experts * MAIN
    first = near.shape[1]

    def kernel(slot_ref, near_ref, far_ref, residual_ref, gain_ref, out_ref, hidden_ref, normed):
        step = pl.program_id(0)

        @pl.when(step == 0)
        def _():
            hidden_ref[:, :first] = residual_ref[:, :first].astype(F32) + near_ref[...]
            hidden_ref[:, first:] = residual_ref[:, first:].astype(F32) + far_ref[...]
            hidden = hidden_ref[...]
            inv_rms = lax.rsqrt(jnp.mean(hidden * hidden, axis=1, keepdims=True) + 1e-06)
            value = (hidden * inv_rms * gain_ref[...]).astype(BF16)
            for c in range(PIECES):
                normed[c] = value[:, c * tile : (c + 1) * tile]

        slots = jnp.broadcast_to(slot_ref[...][:, None, :], (experts, MAIN, toks))
        row = lax.broadcasted_iota(jnp.int32, (experts, MAIN, toks), 1)

        def hot(mask):
            return jnp.where(mask, 1.0, 0.0).reshape(flat, toks).astype(BF16)

        @pl.when(step < PIECES)
        def _():
            out_ref[...] = dot(hot(slots == row), normed[step]).astype(BF16)

        @pl.when(step == PIECES)
        def _():
            spill = slots == MAIN + row // PIECES
            parts = [hot(spill & (row % PIECES == c)) for c in range(PIECES)]
            out_ref[...] = dot(jnp.concatenate(parts, axis=1), normed[...].reshape(PIECES * toks, tile)).astype(BF16)

    whole = lambda i: (0, 0)
    return pl.pallas_call(
        kernel,
        grid=(PIECES + 1,),
        in_specs=[
            pl.BlockSpec(slot.shape, whole),
            pl.BlockSpec(near.shape, whole),
            pl.BlockSpec(far.shape, whole),
            pl.BlockSpec(residual.shape, whole),
            pl.BlockSpec(gain.shape, whole),
        ],
        out_specs=[pl.BlockSpec((flat, tile), lambda i: (0, i)), pl.BlockSpec((toks, width), whole)],
        out_shape=[
            jax.ShapeDtypeStruct((flat, tile * (PIECES + 1)), BF16),
            jax.ShapeDtypeStruct((toks, width), F32),
        ],
        scratch_shapes=[pltpu.VMEM((PIECES, toks, tile), BF16)],
        compiler_params=pltpu.CompilerParams(vmem_limit_bytes=VMEM),
        cost_estimate=pl.CostEstimate(flops=3 * 10**9, bytes_accessed=15 * 10**6, transcendentals=0),
        name="build_rows",
    )(slot, near, far, residual, gain)


def silu_times(gate, up):
    return (gate * jax.nn.sigmoid(gate) * up).astype(BF16)


def expert(got, w_gate, w_up, w_down, block=256):
    flat, columns = got.shape
    width, hid = w_gate.shape
    tile = columns - width
    extra = block // PIECES

    def kernel(got_ref, gate_ref, up_ref, down_ref, out_ref, rows, spill):
        rows[:block] = got_ref[:, :width]
        for c in range(tile // LANES):
            spill[c] = got_ref[:, width + c * LANES : width + (c + 1) * LANES].astype(F32)
        for c in range(PIECES):
            for d in range(tile // LANES):
                at = c * tile + d * LANES
                rows[block:, at : at + LANES] = spill[d, pl.ds(c, extra, stride=PIECES), :].astype(BF16)
        value = rows[...]
        active = silu_times(dot(value, gate_ref[...]), dot(value, up_ref[...]))
        for c in range(PIECES):
            cols = slice(c * tile, (c + 1) * tile)
            made = dot(active, down_ref[:, cols])
            out_ref[:, cols] = made[:block].astype(BF16)
            for d in range(tile // LANES):
                spill[d, pl.ds(c, extra, stride=PIECES), :] = made[block:, d * LANES : (d + 1) * LANES]
        for d in range(tile // LANES):
            out_ref[:, width + d * LANES : width + (d + 1) * LANES] = spill[d].astype(BF16)

    whole = lambda i: (0, 0)
    once = pl.Buffered(1)
    return pl.pallas_call(
        kernel,
        grid=(flat // block,),
        in_specs=[
            pl.BlockSpec((block, columns), lambda i: (i, 0)),
            pl.BlockSpec((width, hid), whole, pipeline_mode=once),
            pl.BlockSpec((width, hid), whole, pipeline_mode=once),
            pl.BlockSpec((hid, width), whole, pipeline_mode=once),
        ],
        out_specs=pl.BlockSpec((block, columns), lambda i: (i, 0)),
        out_shape=jax.ShapeDtypeStruct((flat, columns), BF16),
        scratch_shapes=[
            pltpu.VMEM((block + extra, width), BF16),
            pltpu.VMEM((tile // LANES, block, LANES), F32),
        ],
        compiler_params=pltpu.CompilerParams(vmem_limit_bytes=30 * 2**20),
        cost_estimate=pl.CostEstimate(flops=24 * 10**9, bytes_accessed=40 * 10**6, transcendentals=10**6),
        name="expert_rows",
    )(got, w_gate, w_up, w_down)


def combine(main_w, spill_w, back, hidden):
    toks, width = hidden.shape
    flat = back.shape[0]
    halves = 2
    tile = (back.shape[1] - width) // halves
    tiles = width // tile

    few = flat // PIECES

    def kernel(main_w_ref, spill_w_ref, main_ref, spill_ref, hidden_ref, out_ref, spill, rows):
        piece = pl.program_id(1)

        @pl.when(piece == 0)
        def _():
            for d in range(tile // LANES):
                spill[d] = spill_ref[:, d * LANES : (d + 1) * LANES].astype(F32)
            for c in range(PIECES):
                for d in range(tile // LANES):
                    picked = spill[d, pl.ds(c, few, stride=PIECES), :]
                    rows[c, :, d * LANES : (d + 1) * LANES] = picked.astype(BF16)

        both = dot(main_w_ref[...], main_ref[...]) + dot(spill_w_ref[...], rows[piece])
        out_ref[...] = (hidden_ref[...] + (both[:toks] + both[toks:])).astype(BF16)

    along = lambda half, piece: (0, piece * halves + half)
    return pl.pallas_call(
        kernel,
        grid=(halves, PIECES),
        in_specs=[
            pl.BlockSpec((2 * toks, flat), lambda half, piece: (0, 0)),
            pl.BlockSpec((2 * toks, few), lambda half, piece: (0, 0)),
            pl.BlockSpec((flat, tile), along),
            pl.BlockSpec((flat, tile), lambda half, piece: (0, tiles + half)),
            pl.BlockSpec((toks, tile), along),
        ],
        out_specs=pl.BlockSpec((toks, tile), along),
        out_shape=jax.ShapeDtypeStruct((toks, width), BF16),
        scratch_shapes=[
            pltpu.VMEM((tile // LANES, flat, LANES), F32),
            pltpu.VMEM((PIECES, few, tile), BF16),
        ],
        compiler_params=pltpu.CompilerParams(vmem_limit_bytes=16 * 2**20),
        cost_estimate=pl.CostEstimate(flops=4 * 10**9, bytes_accessed=15 * 10**6, transcendentals=0),
        name="combine_rows",
    )(main_w, spill_w, back, back, hidden)


def project_scatter(attn_heads, out_weight, toks):
    width = out_weight.shape[1]
    first = width * 5 // 8
    at = lax.axis_index("tensor")
    x, z = at // 2, at % 2
    heads = attn_heads.reshape(4, 2, toks, attn_heads.shape[1])

    def along_x(v, by):
        return lax.ppermute(v, "tensor", [(i * 2 + j, (i + by) % 4 * 2 + j) for i in range(4) for j in range(2)])

    def along_z(v):
        return lax.ppermute(v, "tensor", [(i, i ^ 1) for i in range(8)])

    def times(rows, lo, hi):
        return dot(rows, out_weight[:, lo:hi]).astype(BF16)

    def pick(v, i):
        return lax.dynamic_index_in_dim(v, i, 0, keepdims=False)

    def add(a, b):
        return (a.astype(F32) + b.astype(F32)).astype(BF16)

    by_z = heads.swapaxes(0, 1)
    far_rows = [pick(heads, (x + d) % 4).reshape(2 * toks, -1) for d in range(4)]
    mid = first // 2

    up_two, down_two = times(far_rows[2], mid, first), times(far_rows[2], 0, mid)
    z_rows = pick(by_z, 1 - z).reshape(4 * toks, -1)
    up_two, down_two, z_rows = lax.optimization_barrier((up_two, down_two, z_rows))
    up_far, down_far = along_x(up_two, 1), along_x(down_two, -1)
    away = along_z(times(z_rows, first, width))
    up_near = along_x(times(far_rows[1], 0, mid), 1)
    down_near = along_x(times(far_rows[3], mid, first), -1)
    up_sum = along_x(add(dot(far_rows[1], out_weight[:, mid:first]).astype(BF16), up_far), 1)
    down_sum = along_x(add(dot(far_rows[3], out_weight[:, :mid]).astype(BF16), down_far), -1)

    own = times(pick(by_z, z).reshape(4 * toks, -1), first, width)
    both = add(own, away)
    both, own_rows = lax.optimization_barrier((both, far_rows[0]))
    both = both.reshape(4, toks, width - first)
    chunk = [pick(both, (x + d) % 4) for d in range(4)]
    half = (width - first) // 2
    b_up_far, b_down_far = along_x(chunk[2][:, half:], 1), along_x(chunk[2][:, :half], -1)
    b_up_near, b_down_near = along_x(chunk[1][:, :half], 1), along_x(chunk[3][:, half:], -1)
    b_up_sum = along_x(add(chunk[1][:, half:], b_up_far), 1)
    b_down_sum = along_x(add(chunk[3][:, :half], b_down_far), -1)

    left = times(own_rows, 0, mid).astype(F32) + up_near.astype(F32) + down_sum.astype(F32)
    right = times(own_rows, mid, first).astype(F32) + up_sum.astype(F32) + down_near.astype(F32)
    near = jnp.concatenate([left, right], axis=1).reshape(2, toks, first)
    near = pick(near, z) + along_z(pick(near, 1 - z).astype(BF16)).astype(F32)
    b_left = chunk[0][:, :half].astype(F32) + b_up_near.astype(F32) + b_down_sum.astype(F32)
    b_right = chunk[0][:, half:].astype(F32) + b_up_sum.astype(F32) + b_down_near.astype(F32)
    return near, jnp.concatenate([b_left, b_right], axis=1)


def shards(attn_heads, out_weight, residual, norm_gain, expert_ids, gate_probs, expert_gate, expert_up, expert_down):
    toks, width = residual.shape
    experts = lax.axis_size("dp") * lax.axis_size("tensor")
    flat = experts * MAIN
    slot, prob = route(expert_ids, gate_probs, experts)
    main_w, spill_w = combine_weights(slot, prob)
    near, far = project_scatter(attn_heads, out_weight, toks)
    near, main_w, spill_w = lax.optimization_barrier((near, main_w, spill_w))
    sent, hidden = build(slot, near, far, residual, norm_gain[None, :])

    def swap(v):
        cols = v.shape[1]
        v = lax.all_to_all(v.reshape(experts, MAIN, cols), ("dp", "tensor"), split_axis=0, concat_axis=0, tiled=True)
        return v.reshape(flat, cols)

    made = expert(swap(sent), expert_gate[0], expert_up[0], expert_down[0])
    return combine(main_w, spill_w, swap(made), hidden)


def solution(mesh):
    both = ("dp", "tensor")
    in_specs = (
        P("dp", "tensor"),
        P("tensor", None),
        P(both, None),
        P(),
        P(both, None),
        P(both, None),
        P(both, None, None),
        P(both, None, None),
        P(both, None, None),
    )
    return jax.shard_map(shards, mesh=mesh, in_specs=in_specs, out_specs=P(both, None), check_vma=False)
```

```python
import jax
import jax.numpy as jnp
from jax import lax
from jax.experimental import pallas as pl
from jax.experimental.pallas import tpu as pltpu
from jax.sharding import PartitionSpec as P

F32, BF16 = jnp.float32, jnp.bfloat16
MAIN = 8
PIECES = 4
LANES = 128
VMEM = 40 * 2**20


def dot(a, b):
    return jnp.dot(a, b, preferred_element_type=F32)


def route(expert_ids, gate_probs, experts):
    toks = expert_ids.shape[0]
    names = jnp.arange(experts, dtype=jnp.int32)
    chosen = expert_ids.T[:, None, :] == names[None, :, None]
    taken = jnp.any(chosen, axis=0)
    prob = jnp.sum(jnp.where(chosen, gate_probs.T[:, None, :], 0.0), axis=0)
    order = jnp.arange(toks)
    earlier = (order[:, None] < order[None, :]).astype(BF16)
    before = dot(taken.astype(BF16), earlier)
    return jnp.where(taken, before.astype(jnp.int32), -1), prob


def combine_weights(slot, prob):
    experts, toks = slot.shape
    hi = prob.astype(BF16)
    lo = (prob - hi.astype(F32)).astype(BF16)
    both = jnp.concatenate([hi, lo], axis=1)

    def spread(names):
        hot = slot[:, None, :] == names[None, :, None]
        hot = jnp.concatenate([hot, hot], axis=2)
        return jnp.where(hot, both[:, None, :], jnp.zeros((), BF16)).reshape(experts * names.size, 2 * toks).T

    return spread(jnp.arange(MAIN, dtype=jnp.int32)), spread(MAIN + jnp.arange(MAIN // PIECES, dtype=jnp.int32))


def build(slot, near, far, residual, gain):
    experts, toks = slot.shape
    width = residual.shape[1]
    tile = width // PIECES
    flat = experts * MAIN
    first = near.shape[1]

    def kernel(slot_ref, near_ref, far_ref, residual_ref, gain_ref, out_ref, hidden_ref, normed):
        step = pl.program_id(0)

        @pl.when(step == 0)
        def _():
            hidden_ref[:, :first] = residual_ref[:, :first].astype(F32) + near_ref[...]
            hidden_ref[:, first:] = residual_ref[:, first:].astype(F32) + far_ref[...]
            hidden = hidden_ref[...]
            inv_rms = lax.rsqrt(jnp.mean(hidden * hidden, axis=1, keepdims=True) + 1e-06)
            value = (hidden * inv_rms * gain_ref[...]).astype(BF16)
            for c in range(PIECES):
                normed[c] = value[:, c * tile : (c + 1) * tile]

        slots = jnp.broadcast_to(slot_ref[...][:, None, :], (experts, MAIN, toks))
        row = lax.broadcasted_iota(jnp.int32, (experts, MAIN, toks), 1)

        def hot(mask):
            return jnp.where(mask, 1.0, 0.0).reshape(flat, toks).astype(BF16)

        @pl.when(step < PIECES)
        def _():
            out_ref[...] = dot(hot(slots == row), normed[step]).astype(BF16)

        @pl.when(step == PIECES)
        def _():
            spill = slots == MAIN + row // PIECES
            parts = [hot(spill & (row % PIECES == c)) for c in range(PIECES)]
            out_ref[...] = dot(jnp.concatenate(parts, axis=1), normed[...].reshape(PIECES * toks, tile)).astype(BF16)

    whole = lambda i: (0, 0)
    return pl.pallas_call(
        kernel,
        grid=(PIECES + 1,),
        in_specs=[
            pl.BlockSpec(slot.shape, whole),
            pl.BlockSpec(near.shape, whole),
            pl.BlockSpec(far.shape, whole),
            pl.BlockSpec(residual.shape, whole),
            pl.BlockSpec(gain.shape, whole),
        ],
        out_specs=[pl.BlockSpec((flat, tile), lambda i: (0, i)), pl.BlockSpec((toks, width), whole)],
        out_shape=[
            jax.ShapeDtypeStruct((flat, tile * (PIECES + 1)), BF16),
            jax.ShapeDtypeStruct((toks, width), F32),
        ],
        scratch_shapes=[pltpu.VMEM((PIECES, toks, tile), BF16)],
        compiler_params=pltpu.CompilerParams(vmem_limit_bytes=26 * 2**20),
        cost_estimate=pl.CostEstimate(flops=3 * 10**9, bytes_accessed=15 * 10**6, transcendentals=0),
        name="build_rows",
    )(slot, near, far, residual, gain)


def silu_times(gate, up):
    return (gate * jax.nn.sigmoid(gate) * up).astype(BF16)


def expert(got, w_gate, w_up, w_down, block=256):
    flat, columns = got.shape
    width, hid = w_gate.shape
    tile = columns - width
    extra = block // PIECES

    def kernel(got_ref, gate_ref, up_ref, down_ref, out_ref, rows, spill):
        rows[:block] = got_ref[:, :width]
        for c in range(tile // LANES):
            spill[c] = got_ref[:, width + c * LANES : width + (c + 1) * LANES].astype(F32)
        for c in range(PIECES):
            for d in range(tile // LANES):
                at = c * tile + d * LANES
                rows[block:, at : at + LANES] = spill[d, pl.ds(c, extra, stride=PIECES), :].astype(BF16)
        value = rows[...]
        active = silu_times(dot(value, gate_ref[...]), dot(value, up_ref[...]))
        for c in range(PIECES):
            cols = slice(c * tile, (c + 1) * tile)
            made = dot(active, down_ref[:, cols])
            out_ref[:, cols] = made[:block].astype(BF16)
            for d in range(tile // LANES):
                spill[d, pl.ds(c, extra, stride=PIECES), :] = made[block:, d * LANES : (d + 1) * LANES]
        for d in range(tile // LANES):
            out_ref[:, width + d * LANES : width + (d + 1) * LANES] = spill[d].astype(BF16)

    whole = lambda i: (0, 0)
    once = pl.Buffered(1)
    return pl.pallas_call(
        kernel,
        grid=(flat // block,),
        in_specs=[
            pl.BlockSpec((block, columns), lambda i: (i, 0)),
            pl.BlockSpec((width, hid), whole, pipeline_mode=once),
            pl.BlockSpec((width, hid), whole, pipeline_mode=once),
            pl.BlockSpec((hid, width), whole, pipeline_mode=once),
        ],
        out_specs=pl.BlockSpec((block, columns), lambda i: (i, 0)),
        out_shape=jax.ShapeDtypeStruct((flat, columns), BF16),
        scratch_shapes=[
            pltpu.VMEM((block + extra, width), BF16),
            pltpu.VMEM((tile // LANES, block, LANES), F32),
        ],
        compiler_params=pltpu.CompilerParams(vmem_limit_bytes=30 * 2**20),
        cost_estimate=pl.CostEstimate(flops=24 * 10**9, bytes_accessed=40 * 10**6, transcendentals=10**6),
        name="expert_rows",
    )(got, w_gate, w_up, w_down)


def combine(main_w, spill_w, back, hidden):
    toks, width = hidden.shape
    flat = back.shape[0]
    halves = 2
    tile = (back.shape[1] - width) // halves
    tiles = width // tile

    few = flat // PIECES

    def kernel(main_w_ref, spill_w_ref, main_ref, spill_ref, hidden_ref, out_ref, spill, rows):
        piece = pl.program_id(1)

        @pl.when(piece == 0)
        def _():
            for d in range(tile // LANES):
                spill[d] = spill_ref[:, d * LANES : (d + 1) * LANES].astype(F32)
            for c in range(PIECES):
                for d in range(tile // LANES):
                    picked = spill[d, pl.ds(c, few, stride=PIECES), :]
                    rows[c, :, d * LANES : (d + 1) * LANES] = picked.astype(BF16)

        both = dot(main_w_ref[...], main_ref[...]) + dot(spill_w_ref[...], rows[piece])
        out_ref[...] = (hidden_ref[...] + (both[:toks] + both[toks:])).astype(BF16)

    along = lambda half, piece: (0, piece * halves + half)
    return pl.pallas_call(
        kernel,
        grid=(halves, PIECES),
        in_specs=[
            pl.BlockSpec((2 * toks, flat), lambda half, piece: (0, 0)),
            pl.BlockSpec((2 * toks, few), lambda half, piece: (0, 0)),
            pl.BlockSpec((flat, tile), along),
            pl.BlockSpec((flat, tile), lambda half, piece: (0, tiles + half)),
            pl.BlockSpec((toks, tile), along),
        ],
        out_specs=pl.BlockSpec((toks, tile), along),
        out_shape=jax.ShapeDtypeStruct((toks, width), BF16),
        scratch_shapes=[
            pltpu.VMEM((tile // LANES, flat, LANES), F32),
            pltpu.VMEM((PIECES, few, tile), BF16),
        ],
        compiler_params=pltpu.CompilerParams(vmem_limit_bytes=16 * 2**20),
        cost_estimate=pl.CostEstimate(flops=4 * 10**9, bytes_accessed=15 * 10**6, transcendentals=0),
        name="combine_rows",
    )(main_w, spill_w, back, back, hidden)


def project_scatter(attn_heads, out_weight, toks):
    width = out_weight.shape[1]
    first = width * 5 // 8
    at = lax.axis_index("tensor")
    x, z = at // 2, at % 2
    heads = attn_heads.reshape(4, 2, toks, attn_heads.shape[1])

    def along_x(v, by):
        return lax.ppermute(v, "tensor", [(i * 2 + j, (i + by) % 4 * 2 + j) for i in range(4) for j in range(2)])

    def along_z(v):
        return lax.ppermute(v, "tensor", [(i, i ^ 1) for i in range(8)])

    def times(rows, lo, hi):
        return dot(rows, out_weight[:, lo:hi]).astype(BF16)

    def pick(v, i):
        return lax.dynamic_index_in_dim(v, i, 0, keepdims=False)

    def add(a, b):
        return (a.astype(F32) + b.astype(F32)).astype(BF16)

    by_z = heads.swapaxes(0, 1)
    far_rows = [pick(heads, (x + d) % 4).reshape(2 * toks, -1) for d in range(4)]
    mid = first // 2

    up_two, down_two = times(far_rows[2], mid, first), times(far_rows[2], 0, mid)
    z_rows = pick(by_z, 1 - z).reshape(4 * toks, -1)
    up_two, down_two, z_rows = lax.optimization_barrier((up_two, down_two, z_rows))
    z_chunk = times(z_rows, first, width)
    z_chunk, up_rows, down_rows = lax.optimization_barrier((z_chunk, far_rows[1], far_rows[3]))
    up_one, down_one = times(up_rows, 0, mid), times(down_rows, mid, first)
    up_one, down_one, up_rows, down_rows = lax.optimization_barrier((up_one, down_one, up_rows, down_rows))
    up_far, down_far = along_x(up_two, 1), along_x(down_two, -1)
    away = along_z(z_chunk)
    up_near, down_near = along_x(up_one, 1), along_x(down_one, -1)
    up_sum = along_x(add(times(up_rows, mid, first), up_far), 1)
    down_sum = along_x(add(times(down_rows, 0, mid), down_far), -1)

    own = times(pick(by_z, z).reshape(4 * toks, -1), first, width)
    both = add(own, away)
    both, own_rows = lax.optimization_barrier((both, far_rows[0]))
    both = both.reshape(4, toks, width - first)
    chunk = [pick(both, (x + d) % 4) for d in range(4)]
    from_down, from_up, from_two = along_x(chunk[1], 1), along_x(chunk[3], -1), along_x(chunk[2], 2)

    left = times(own_rows, 0, mid).astype(F32) + up_near.astype(F32) + down_sum.astype(F32)
    right = times(own_rows, mid, first).astype(F32) + up_sum.astype(F32) + down_near.astype(F32)
    near = jnp.concatenate([left, right], axis=1).reshape(2, toks, first)
    near = pick(near, z) + along_z(pick(near, 1 - z).astype(BF16)).astype(F32)
    far = chunk[0].astype(F32) + from_down.astype(F32) + from_up.astype(F32) + from_two.astype(F32)
    return near, far


def shards(attn_heads, out_weight, residual, norm_gain, expert_ids, gate_probs, expert_gate, expert_up, expert_down):
    toks, width = residual.shape
    experts = lax.axis_size("dp") * lax.axis_size("tensor")
    flat = experts * MAIN
    slot, prob = route(expert_ids, gate_probs, experts)
    main_w, spill_w = combine_weights(slot, prob)
    near, far = project_scatter(attn_heads, out_weight, toks)
    near, main_w, spill_w = lax.optimization_barrier((near, main_w, spill_w))
    sent, hidden = build(slot, near, far, residual, norm_gain[None, :])

    def swap(v):
        cols = v.shape[1]
        v = lax.all_to_all(v.reshape(experts, MAIN, cols), ("dp", "tensor"), split_axis=0, concat_axis=0, tiled=True)
        return v.reshape(flat, cols)

    made = expert(swap(sent), expert_gate[0], expert_up[0], expert_down[0])
    return combine(main_w, spill_w, swap(made), hidden)


def solution(mesh):
    both = ("dp", "tensor")
    in_specs = (
        P("dp", "tensor"),
        P("tensor", None),
        P(both, None),
        P(),
        P(both, None),
        P(both, None),
        P(both, None, None),
        P(both, None, None),
        P(both, None, None),
    )
    return jax.shard_map(shards, mesh=mesh, in_specs=in_specs, out_specs=P(both, None), check_vma=False)
```

```python
import jax
import jax.numpy as jnp
from jax import lax
from jax.experimental import pallas as pl
from jax.experimental.pallas import tpu as pltpu
from jax.sharding import PartitionSpec as P

F32, BF16 = jnp.float32, jnp.bfloat16
MAIN = 8
PIECES = 4
LANES = 128
VMEM = 40 * 2**20


def dot(a, b):
    return jnp.dot(a, b, preferred_element_type=F32)


def route(expert_ids, gate_probs, experts):
    toks = expert_ids.shape[0]
    names = jnp.arange(experts, dtype=jnp.int32)
    chosen = expert_ids.T[:, None, :] == names[None, :, None]
    taken = jnp.any(chosen, axis=0)
    prob = jnp.sum(jnp.where(chosen, gate_probs.T[:, None, :], 0.0), axis=0)
    order = jnp.arange(toks)
    earlier = (order[:, None] < order[None, :]).astype(BF16)
    before = dot(taken.astype(BF16), earlier)
    return jnp.where(taken, before.astype(jnp.int32), -1), prob


def combine_weights(slot, prob):
    experts, toks = slot.shape
    hi = prob.astype(BF16)
    lo = (prob - hi.astype(F32)).astype(BF16)
    both = jnp.concatenate([hi, lo], axis=1)

    def spread(names):
        hot = slot[:, None, :] == names[None, :, None]
        hot = jnp.concatenate([hot, hot], axis=2)
        return jnp.where(hot, both[:, None, :], jnp.zeros((), BF16)).reshape(experts * names.size, 2 * toks).T

    return spread(jnp.arange(MAIN, dtype=jnp.int32)), spread(MAIN + jnp.arange(MAIN // PIECES, dtype=jnp.int32))


def build(slot, near, far, residual, gain):
    experts, toks = slot.shape
    width = residual.shape[1]
    tile = width // PIECES
    flat = experts * MAIN
    first = near.shape[1]

    def kernel(slot_ref, near_ref, far_ref, residual_ref, gain_ref, out_ref, hidden_ref, normed):
        step = pl.program_id(0)

        @pl.when(step == 0)
        def _():
            hidden_ref[:, :first] = residual_ref[:, :first].astype(F32) + near_ref[...]
            hidden_ref[:, first:] = residual_ref[:, first:].astype(F32) + far_ref[...]
            hidden = hidden_ref[...]
            inv_rms = lax.rsqrt(jnp.mean(hidden * hidden, axis=1, keepdims=True) + 1e-06)
            value = (hidden * inv_rms * gain_ref[...]).astype(BF16)
            for c in range(PIECES):
                normed[c] = value[:, c * tile : (c + 1) * tile]

        slots = jnp.broadcast_to(slot_ref[...][:, None, :], (experts, MAIN, toks))
        row = lax.broadcasted_iota(jnp.int32, (experts, MAIN, toks), 1)

        def hot(mask):
            return jnp.where(mask, 1.0, 0.0).reshape(flat, toks).astype(BF16)

        @pl.when(step < PIECES)
        def _():
            out_ref[...] = dot(hot(slots == row), normed[step]).astype(BF16)

        @pl.when(step == PIECES)
        def _():
            spill = slots == MAIN + row // PIECES
            parts = [hot(spill & (row % PIECES == c)) for c in range(PIECES)]
            out_ref[...] = dot(jnp.concatenate(parts, axis=1), normed[...].reshape(PIECES * toks, tile)).astype(BF16)

    whole = lambda i: (0, 0)
    return pl.pallas_call(
        kernel,
        grid=(PIECES + 1,),
        in_specs=[
            pl.BlockSpec(slot.shape, whole),
            pl.BlockSpec(near.shape, whole),
            pl.BlockSpec(far.shape, whole),
            pl.BlockSpec(residual.shape, whole),
            pl.BlockSpec(gain.shape, whole),
        ],
        out_specs=[pl.BlockSpec((flat, tile), lambda i: (0, i)), pl.BlockSpec((toks, width), whole)],
        out_shape=[
            jax.ShapeDtypeStruct((flat, tile * (PIECES + 1)), BF16),
            jax.ShapeDtypeStruct((toks, width), F32),
        ],
        scratch_shapes=[pltpu.VMEM((PIECES, toks, tile), BF16)],
        compiler_params=pltpu.CompilerParams(vmem_limit_bytes=26 * 2**20),
        cost_estimate=pl.CostEstimate(flops=3 * 10**9, bytes_accessed=15 * 10**6, transcendentals=0),
        name="build_rows",
    )(slot, near, far, residual, gain)


def silu_times(gate, up):
    return (gate * jax.nn.sigmoid(gate) * up).astype(BF16)


def expert(got, w_gate, w_up, w_down, block=256):
    flat, columns = got.shape
    width, hid = w_gate.shape
    tile = columns - width
    extra = block // PIECES

    def kernel(got_ref, gate_ref, up_ref, down_ref, out_ref, rows, spill):
        rows[:block] = got_ref[:, :width]
        for c in range(tile // LANES):
            spill[c] = got_ref[:, width + c * LANES : width + (c + 1) * LANES].astype(F32)
        for c in range(PIECES):
            for d in range(tile // LANES):
                at = c * tile + d * LANES
                rows[block:, at : at + LANES] = spill[d, pl.ds(c, extra, stride=PIECES), :].astype(BF16)
        value = rows[...]
        active = silu_times(dot(value, gate_ref[...]), dot(value, up_ref[...]))
        for c in range(PIECES):
            cols = slice(c * tile, (c + 1) * tile)
            made = dot(active, down_ref[:, cols])
            out_ref[:, cols] = made[:block].astype(BF16)
            for d in range(tile // LANES):
                spill[d, pl.ds(c, extra, stride=PIECES), :] = made[block:, d * LANES : (d + 1) * LANES]
        for d in range(tile // LANES):
            out_ref[:, width + d * LANES : width + (d + 1) * LANES] = spill[d].astype(BF16)

    whole = lambda i: (0, 0)
    once = pl.Buffered(1)
    return pl.pallas_call(
        kernel,
        grid=(flat // block,),
        in_specs=[
            pl.BlockSpec((block, columns), lambda i: (i, 0)),
            pl.BlockSpec((width, hid), whole, pipeline_mode=once),
            pl.BlockSpec((width, hid), whole, pipeline_mode=once),
            pl.BlockSpec((hid, width), whole, pipeline_mode=once),
        ],
        out_specs=pl.BlockSpec((block, columns), lambda i: (i, 0)),
        out_shape=jax.ShapeDtypeStruct((flat, columns), BF16),
        scratch_shapes=[
            pltpu.VMEM((block + extra, width), BF16),
            pltpu.VMEM((tile // LANES, block, LANES), F32),
        ],
        compiler_params=pltpu.CompilerParams(vmem_limit_bytes=30 * 2**20),
        cost_estimate=pl.CostEstimate(flops=24 * 10**9, bytes_accessed=40 * 10**6, transcendentals=10**6),
        name="expert_rows",
    )(got, w_gate, w_up, w_down)


def combine(main_w, spill_w, back, hidden):
    toks, width = hidden.shape
    flat = back.shape[0]
    halves = 2
    tile = (back.shape[1] - width) // halves
    tiles = width // tile

    few = flat // PIECES

    def kernel(main_w_ref, spill_w_ref, main_ref, spill_ref, hidden_ref, out_ref, spill, rows):
        piece = pl.program_id(1)

        @pl.when(piece == 0)
        def _():
            for d in range(tile // LANES):
                spill[d] = spill_ref[:, d * LANES : (d + 1) * LANES].astype(F32)
            for c in range(PIECES):
                for d in range(tile // LANES):
                    picked = spill[d, pl.ds(c, few, stride=PIECES), :]
                    rows[c, :, d * LANES : (d + 1) * LANES] = picked.astype(BF16)

        both = dot(main_w_ref[...], main_ref[...]) + dot(spill_w_ref[...], rows[piece])
        out_ref[...] = (hidden_ref[...] + (both[:toks] + both[toks:])).astype(BF16)

    along = lambda half, piece: (0, piece * halves + half)
    return pl.pallas_call(
        kernel,
        grid=(halves, PIECES),
        in_specs=[
            pl.BlockSpec((2 * toks, flat), lambda half, piece: (0, 0)),
            pl.BlockSpec((2 * toks, few), lambda half, piece: (0, 0)),
            pl.BlockSpec((flat, tile), along),
            pl.BlockSpec((flat, tile), lambda half, piece: (0, tiles + half)),
            pl.BlockSpec((toks, tile), along),
        ],
        out_specs=pl.BlockSpec((toks, tile), along),
        out_shape=jax.ShapeDtypeStruct((toks, width), BF16),
        scratch_shapes=[
            pltpu.VMEM((tile // LANES, flat, LANES), F32),
            pltpu.VMEM((PIECES, few, tile), BF16),
        ],
        compiler_params=pltpu.CompilerParams(vmem_limit_bytes=16 * 2**20),
        cost_estimate=pl.CostEstimate(flops=4 * 10**9, bytes_accessed=15 * 10**6, transcendentals=0),
        name="combine_rows",
    )(main_w, spill_w, back, back, hidden)


def project_scatter(attn_heads, out_weight, toks):
    width = out_weight.shape[1]
    first = width * 5 // 8
    at = lax.axis_index("tensor")
    x, z = at // 2, at % 2
    heads = attn_heads.reshape(4, 2, toks, attn_heads.shape[1])

    def along_x(v, by):
        return lax.ppermute(v, "tensor", [(i * 2 + j, (i + by) % 4 * 2 + j) for i in range(4) for j in range(2)])

    def along_z(v):
        return lax.ppermute(v, "tensor", [(i, i ^ 1) for i in range(8)])

    def times(rows, lo, hi):
        return dot(rows, out_weight[:, lo:hi]).astype(BF16)

    def pick(v, i):
        return lax.dynamic_index_in_dim(v, i, 0, keepdims=False)

    def add(a, b):
        return (a.astype(F32) + b.astype(F32)).astype(BF16)

    by_z = heads.swapaxes(0, 1)
    far_rows = [pick(heads, (x + d) % 4).reshape(2 * toks, -1) for d in range(4)]
    mid = first // 2

    up_two, down_two = times(far_rows[2], mid, first), times(far_rows[2], 0, mid)
    z_rows = pick(by_z, 1 - z).reshape(4 * toks, -1)
    up_two, down_two, z_rows = lax.optimization_barrier((up_two, down_two, z_rows))
    z_chunk = times(z_rows, first, width)
    up_far, down_far = along_x(up_two, 1), along_x(down_two, -1)
    away = along_z(z_chunk)
    z_chunk, up_rows, down_rows = lax.optimization_barrier((z_chunk, far_rows[1], far_rows[3]))
    up_one, down_one = dot(up_rows, out_weight[:, :first]), dot(down_rows, out_weight[:, :first])
    up_one, down_one, up_far, down_far = lax.optimization_barrier((up_one, down_one, up_far, down_far))
    up_got = along_x(jnp.concatenate([up_one[:, :mid], up_one[:, mid:] + up_far.astype(F32)], axis=1).astype(BF16), 1)
    down_got = along_x(jnp.concatenate([down_one[:, :mid] + down_far.astype(F32), down_one[:, mid:]], axis=1).astype(BF16), -1)

    own = times(pick(by_z, z).reshape(4 * toks, -1), first, width)
    both = add(own, away)
    both, own_rows = lax.optimization_barrier((both, far_rows[0]))
    both = both.reshape(4, toks, width - first)
    chunk = [pick(both, (x + d) % 4) for d in range(4)]
    from_down, from_up, from_two = along_x(chunk[1], 1), along_x(chunk[3], -1), along_x(chunk[2], 2)

    near = times(own_rows, 0, first).astype(F32) + up_got.astype(F32) + down_got.astype(F32)
    near = near.reshape(2, toks, first)
    near = pick(near, z) + along_z(pick(near, 1 - z).astype(BF16)).astype(F32)
    far = chunk[0].astype(F32) + from_down.astype(F32) + from_up.astype(F32) + from_two.astype(F32)
    return near, far


def shards(attn_heads, out_weight, residual, norm_gain, expert_ids, gate_probs, expert_gate, expert_up, expert_down):
    toks, width = residual.shape
    experts = lax.axis_size("dp") * lax.axis_size("tensor")
    flat = experts * MAIN
    slot, prob = route(expert_ids, gate_probs, experts)
    main_w, spill_w = combine_weights(slot, prob)
    near, far = project_scatter(attn_heads, out_weight, toks)
    near, main_w, spill_w = lax.optimization_barrier((near, main_w, spill_w))
    sent, hidden = build(slot, near, far, residual, norm_gain[None, :])

    def swap(v):
        cols = v.shape[1]
        v = lax.all_to_all(v.reshape(experts, MAIN, cols), ("dp", "tensor"), split_axis=0, concat_axis=0, tiled=True)
        return v.reshape(flat, cols)

    made = expert(swap(sent), expert_gate[0], expert_up[0], expert_down[0])
    return combine(main_w, spill_w, swap(made), hidden)


def solution(mesh):
    both = ("dp", "tensor")
    in_specs = (
        P("dp", "tensor"),
        P("tensor", None),
        P(both, None),
        P(),
        P(both, None),
        P(both, None),
        P(both, None, None),
        P(both, None, None),
        P(both, None, None),
    )
    return jax.shard_map(shards, mesh=mesh, in_specs=in_specs, out_specs=P(both, None), check_vma=False)
```

```python
import jax
import jax.numpy as jnp
from jax import lax
from jax.experimental import pallas as pl
from jax.experimental.pallas import tpu as pltpu
from jax.sharding import PartitionSpec as P

F32, BF16 = jnp.float32, jnp.bfloat16
MAIN = 8
PIECES = 4
LANES = 128
VMEM = 40 * 2**20


def dot(a, b):
    return jnp.dot(a, b, preferred_element_type=F32)


def route(expert_ids, gate_probs, experts):
    toks = expert_ids.shape[0]
    names = jnp.arange(experts, dtype=jnp.int32)
    chosen = expert_ids.T[:, None, :] == names[None, :, None]
    taken = jnp.any(chosen, axis=0)
    prob = jnp.sum(jnp.where(chosen, gate_probs.T[:, None, :], 0.0), axis=0)
    order = jnp.arange(toks)
    earlier = (order[:, None] < order[None, :]).astype(BF16)
    before = dot(taken.astype(BF16), earlier)
    return jnp.where(taken, before.astype(jnp.int32), -1), prob


def combine_weights(slot, prob):
    experts, toks = slot.shape
    hi = prob.astype(BF16)
    lo = (prob - hi.astype(F32)).astype(BF16)
    both = jnp.concatenate([hi, lo], axis=1)

    def spread(names):
        hot = slot[:, None, :] == names[None, :, None]
        hot = jnp.concatenate([hot, hot], axis=2)
        return jnp.where(hot, both[:, None, :], jnp.zeros((), BF16)).reshape(experts * names.size, 2 * toks).T

    return spread(jnp.arange(MAIN, dtype=jnp.int32)), spread(MAIN + jnp.arange(MAIN // PIECES, dtype=jnp.int32))


def build(slot, near, far, residual, gain):
    experts, toks = slot.shape
    width = residual.shape[1]
    tile = width // PIECES
    flat = experts * MAIN
    first = near.shape[1]

    def kernel(slot_ref, near_ref, far_ref, residual_ref, gain_ref, out_ref, hidden_ref, normed):
        step = pl.program_id(0)

        @pl.when(step == 0)
        def _():
            hidden_ref[:, :first] = residual_ref[:, :first].astype(F32) + near_ref[...]
            hidden_ref[:, first:] = residual_ref[:, first:].astype(F32) + far_ref[...]
            hidden = hidden_ref[...]
            inv_rms = lax.rsqrt(jnp.mean(hidden * hidden, axis=1, keepdims=True) + 1e-06)
            value = (hidden * inv_rms * gain_ref[...]).astype(BF16)
            for c in range(PIECES):
                normed[c] = value[:, c * tile : (c + 1) * tile]

        slots = jnp.broadcast_to(slot_ref[...][:, None, :], (experts, MAIN, toks))
        row = lax.broadcasted_iota(jnp.int32, (experts, MAIN, toks), 1)

        def hot(mask):
            return jnp.where(mask, 1.0, 0.0).reshape(flat, toks).astype(BF16)

        @pl.when(step < PIECES)
        def _():
            out_ref[...] = dot(hot(slots == row), normed[step]).astype(BF16)

        @pl.when(step == PIECES)
        def _():
            spill = slots == MAIN + row // PIECES
            parts = [hot(spill & (row % PIECES == c)) for c in range(PIECES)]
            out_ref[...] = dot(jnp.concatenate(parts, axis=1), normed[...].reshape(PIECES * toks, tile)).astype(BF16)

    whole = lambda i: (0, 0)
    return pl.pallas_call(
        kernel,
        grid=(PIECES + 1,),
        in_specs=[
            pl.BlockSpec(slot.shape, whole),
            pl.BlockSpec(near.shape, whole),
            pl.BlockSpec(far.shape, whole),
            pl.BlockSpec(residual.shape, whole),
            pl.BlockSpec(gain.shape, whole),
        ],
        out_specs=[pl.BlockSpec((flat, tile), lambda i: (0, i)), pl.BlockSpec((toks, width), whole)],
        out_shape=[
            jax.ShapeDtypeStruct((flat, tile * (PIECES + 1)), BF16),
            jax.ShapeDtypeStruct((toks, width), F32),
        ],
        scratch_shapes=[pltpu.VMEM((PIECES, toks, tile), BF16)],
        compiler_params=pltpu.CompilerParams(vmem_limit_bytes=26 * 2**20),
        cost_estimate=pl.CostEstimate(flops=3 * 10**9, bytes_accessed=15 * 10**6, transcendentals=0),
        name="build_rows",
    )(slot, near, far, residual, gain)


def silu_times(gate, up):
    return (gate * jax.nn.sigmoid(gate) * up).astype(BF16)


def expert(got, w_gate, w_up, w_down, block=256):
    flat, columns = got.shape
    width, hid = w_gate.shape
    tile = columns - width
    extra = block // PIECES

    def kernel(got_ref, gate_ref, up_ref, down_ref, out_ref, rows, spill):
        rows[:block] = got_ref[:, :width]
        for c in range(tile // LANES):
            spill[c] = got_ref[:, width + c * LANES : width + (c + 1) * LANES].astype(F32)
        for c in range(PIECES):
            for d in range(tile // LANES):
                at = c * tile + d * LANES
                rows[block:, at : at + LANES] = spill[d, pl.ds(c, extra, stride=PIECES), :].astype(BF16)
        value = rows[...]
        active = silu_times(dot(value, gate_ref[...]), dot(value, up_ref[...]))
        for c in range(PIECES):
            cols = slice(c * tile, (c + 1) * tile)
            made = dot(active, down_ref[:, cols])
            out_ref[:, cols] = made[:block].astype(BF16)
            for d in range(tile // LANES):
                spill[d, pl.ds(c, extra, stride=PIECES), :] = made[block:, d * LANES : (d + 1) * LANES]
        for d in range(tile // LANES):
            out_ref[:, width + d * LANES : width + (d + 1) * LANES] = spill[d].astype(BF16)

    whole = lambda i: (0, 0)
    once = pl.Buffered(1)
    return pl.pallas_call(
        kernel,
        grid=(flat // block,),
        in_specs=[
            pl.BlockSpec((block, columns), lambda i: (i, 0)),
            pl.BlockSpec((width, hid), whole, pipeline_mode=once),
            pl.BlockSpec((width, hid), whole, pipeline_mode=once),
            pl.BlockSpec((hid, width), whole, pipeline_mode=once),
        ],
        out_specs=pl.BlockSpec((block, columns), lambda i: (i, 0)),
        out_shape=jax.ShapeDtypeStruct((flat, columns), BF16),
        scratch_shapes=[
            pltpu.VMEM((block + extra, width), BF16),
            pltpu.VMEM((tile // LANES, block, LANES), F32),
        ],
        compiler_params=pltpu.CompilerParams(vmem_limit_bytes=30 * 2**20),
        cost_estimate=pl.CostEstimate(flops=24 * 10**9, bytes_accessed=40 * 10**6, transcendentals=10**6),
        name="expert_rows",
    )(got, w_gate, w_up, w_down)


def combine(main_w, spill_w, back, hidden):
    toks, width = hidden.shape
    flat = back.shape[0]
    halves = 2
    tile = (back.shape[1] - width) // halves
    tiles = width // tile

    few = flat // PIECES

    def kernel(main_w_ref, spill_w_ref, main_ref, spill_ref, hidden_ref, out_ref, spill, rows):
        piece = pl.program_id(1)

        @pl.when(piece == 0)
        def _():
            for d in range(tile // LANES):
                spill[d] = spill_ref[:, d * LANES : (d + 1) * LANES].astype(F32)
            for c in range(PIECES):
                for d in range(tile // LANES):
                    picked = spill[d, pl.ds(c, few, stride=PIECES), :]
                    rows[c, :, d * LANES : (d + 1) * LANES] = picked.astype(BF16)

        both = dot(main_w_ref[...], main_ref[...]) + dot(spill_w_ref[...], rows[piece])
        out_ref[...] = (hidden_ref[...] + (both[:toks] + both[toks:])).astype(BF16)

    along = lambda half, piece: (0, piece * halves + half)
    return pl.pallas_call(
        kernel,
        grid=(halves, PIECES),
        in_specs=[
            pl.BlockSpec((2 * toks, flat), lambda half, piece: (0, 0)),
            pl.BlockSpec((2 * toks, few), lambda half, piece: (0, 0)),
            pl.BlockSpec((flat, tile), along),
            pl.BlockSpec((flat, tile), lambda half, piece: (0, tiles + half)),
            pl.BlockSpec((toks, tile), along),
        ],
        out_specs=pl.BlockSpec((toks, tile), along),
        out_shape=jax.ShapeDtypeStruct((toks, width), BF16),
        scratch_shapes=[
            pltpu.VMEM((tile // LANES, flat, LANES), F32),
            pltpu.VMEM((PIECES, few, tile), BF16),
        ],
        compiler_params=pltpu.CompilerParams(vmem_limit_bytes=16 * 2**20),
        cost_estimate=pl.CostEstimate(flops=4 * 10**9, bytes_accessed=15 * 10**6, transcendentals=0),
        name="combine_rows",
    )(main_w, spill_w, back, back, hidden)


def project_scatter(attn_heads, out_weight, toks):
    width = out_weight.shape[1]
    first = width * 9 // 16
    at = lax.axis_index("tensor")
    x, z = at // 2, at % 2
    heads = attn_heads.reshape(4, 2, toks, attn_heads.shape[1])

    def along_x(v, by):
        return lax.ppermute(v, "tensor", [(i * 2 + j, (i + by) % 4 * 2 + j) for i in range(4) for j in range(2)])

    def along_z(v):
        return lax.ppermute(v, "tensor", [(i, i ^ 1) for i in range(8)])

    def times(rows, lo, hi):
        return dot(rows, out_weight[:, lo:hi]).astype(BF16)

    def pick(v, i):
        return lax.dynamic_index_in_dim(v, i, 0, keepdims=False)

    def add(a, b):
        return (a.astype(F32) + b.astype(F32)).astype(BF16)

    by_z = heads.swapaxes(0, 1)
    far_rows = [pick(heads, (x + d) % 4).reshape(2 * toks, -1) for d in range(4)]
    mid = first // 2

    up_two, down_two = times(far_rows[2], mid, first), times(far_rows[2], 0, mid)
    z_rows = pick(by_z, 1 - z).reshape(4 * toks, -1)
    up_two, down_two, z_rows = lax.optimization_barrier((up_two, down_two, z_rows))
    z_chunk = times(z_rows, first, width)
    up_far, down_far = along_x(up_two, 1), along_x(down_two, -1)
    away = along_z(z_chunk)
    z_chunk, up_rows, down_rows = lax.optimization_barrier((z_chunk, far_rows[1], far_rows[3]))
    up_one, down_one = dot(up_rows, out_weight[:, :first]), dot(down_rows, out_weight[:, :first])
    up_one, down_one, up_far, down_far = lax.optimization_barrier((up_one, down_one, up_far, down_far))
    up_got = along_x(jnp.concatenate([up_one[:, :mid], up_one[:, mid:] + up_far.astype(F32)], axis=1).astype(BF16), 1)
    down_got = along_x(jnp.concatenate([down_one[:, :mid] + down_far.astype(F32), down_one[:, mid:]], axis=1).astype(BF16), -1)

    own = times(pick(by_z, z).reshape(4 * toks, -1), first, width)
    both = add(own, away)
    both, own_rows = lax.optimization_barrier((both, far_rows[0]))
    both = both.reshape(4, toks, width - first)
    chunk = [pick(both, (x + d) % 4) for d in range(4)]
    from_down, from_up, from_two = along_x(chunk[1], 1), along_x(chunk[3], -1), along_x(chunk[2], 2)

    near = times(own_rows, 0, first).astype(F32) + up_got.astype(F32) + down_got.astype(F32)
    near = near.reshape(2, toks, first)
    near = pick(near, z) + along_z(pick(near, 1 - z).astype(BF16)).astype(F32)
    far = chunk[0].astype(F32) + from_down.astype(F32) + from_up.astype(F32) + from_two.astype(F32)
    return near, far


def shards(attn_heads, out_weight, residual, norm_gain, expert_ids, gate_probs, expert_gate, expert_up, expert_down):
    toks, width = residual.shape
    experts = lax.axis_size("dp") * lax.axis_size("tensor")
    flat = experts * MAIN
    slot, prob = route(expert_ids, gate_probs, experts)
    main_w, spill_w = combine_weights(slot, prob)
    near, far = project_scatter(attn_heads, out_weight, toks)
    near, main_w, spill_w = lax.optimization_barrier((near, main_w, spill_w))
    sent, hidden = build(slot, near, far, residual, norm_gain[None, :])

    def swap(v):
        cols = v.shape[1]
        v = lax.all_to_all(v.reshape(experts, MAIN, cols), ("dp", "tensor"), split_axis=0, concat_axis=0, tiled=True)
        return v.reshape(flat, cols)

    made = expert(swap(sent), expert_gate[0], expert_up[0], expert_down[0])
    return combine(main_w, spill_w, swap(made), hidden)


def solution(mesh):
    both = ("dp", "tensor")
    in_specs = (
        P("dp", "tensor"),
        P("tensor", None),
        P(both, None),
        P(),
        P(both, None),
        P(both, None),
        P(both, None, None),
        P(both, None, None),
        P(both, None, None),
    )
    return jax.shard_map(shards, mesh=mesh, in_specs=in_specs, out_specs=P(both, None), check_vma=False)
```
